256 devices in a mesh: ki: 8 (over x_hi, y), kj: 32 (over x_lo, z, core).
Axes of the slice: x: 4 (x_hi: 2, x_lo: 2; x = x_hi * 2 + x_lo), y: 4, z: 8, core: 2. Of those that a mesh axis runs over, the one named last changes fastest.
Arguments:
- amps: bfloat16 [8, 32, 8, 4, 400, 400], P('ki', 'kj'), may hold values from -24 to 24
- conserve: int32 [8, 32, 8], P('ki', 'kj'), may hold values from 0 to 7, as said below
Outputs:
- density: float32 [8, 400, 400], P('ki')
The draws below stay inside these ranges and needn't reach their ends.
Inputs may be any that keep to these rules, and one draw needn't show every extreme that they name: For every pair slot (r, s) there is an offset m with conserve[r, s, a] = (m - a) mod 8, so the 8 entries name every block index once and conserve[r, s, conserve[r, s, a]] = a.
All inputs are finite; a program needn't handle non-finite values.
Results may differ from the reference program's by a relative error of at most 0.0003.
Values sent between devices are 32-bit elements; how exact they have to be, the bound alone decides.
No kernel may reach another device: no remote copies, remote signals or barrier semaphores. Data moves between devices by JAX's collectives and lax.ppermute only.
A program may use at most 128 MiB of HBM per device.

```python
import math
import jax
import jax.numpy as jnp
from jax import lax

V = 400
OP = 4
KA = 8
NI = 8
NJ = 32


def pair_offsets(key):
    return jax.random.randint(key, (NI, NJ, 1), 0, KA).astype(jnp.int32)


def draw_conserve(key, part):
    offset = pair_offsets(key)
    blocks = jnp.arange(KA, dtype=jnp.int32)[None, None, :]
    return ((offset - blocks) % KA).astype(jnp.int32)


def assemble(keys, offset, noise, row_scale):
    blocks = jnp.arange(KA, dtype=jnp.int32)[None, None, :]
    partner = ((offset - blocks) % KA).astype(jnp.int32)
    lines = jax.random.normal(keys[2], (KA, V), jnp.float32)
    own_line = lines[None, None, :, None, :, None]
    partner_line = jnp.take(lines, partner, axis=0)[:, :, :, None, None, :]
    pair_weight = jax.random.uniform(keys[3], (NI, NJ, 1, OP, 1, 1), jnp.float32, 0.5, 1.5)
    shared = jax.random.normal(keys[4], (1, 1, KA, 1, V, V), jnp.float32)
    mix_weight = jax.random.uniform(keys[5], (NI, NJ, KA, OP, 1, 1), jnp.float32, -1.5, 1.5)
    rise = jnp.arange(NJ, dtype=jnp.float32)[None, :] / max(NJ - 1, 1)
    jitter = jax.random.uniform(keys[6], (NI, NJ), jnp.float32, -0.25, 0.25)
    pair_scale = jnp.exp(math.log(3.0) * (rise - 0.5) + jitter)[:, :, None, None, None, None]
    shift = jax.random.randint(keys[7], (), 0, KA)
    spiked = (jnp.arange(NI, dtype=jnp.int32)[:, None] + shift) % KA == jnp.arange(KA, dtype=jnp.int32)[None, :]
    spike = jnp.where(spiked, 2.0, 1.0).astype(jnp.float32)[:, None, :, None, None, None]
    values = noise + pair_weight * own_line * partner_line + mix_weight * shared
    values = pair_scale * spike * row_scale * values
    return jnp.clip(values, -24.0, 24.0).astype(jnp.bfloat16)


def draw_amps(key, part):
    offset = pair_offsets(key)
    key = jax.random.fold_in(key, 11)
    keys = jax.random.split(key, 8)
    shape = (NI, NJ, KA, OP, V, V)
    noise = jax.random.normal(keys[0], shape, jnp.float32)
    row_scale = jnp.ones((1, 1, KA, 1, V, 1), jnp.float32)
    return assemble(keys, offset, noise, row_scale)


def setup_inputs(seed: int = 0) -> dict:
    splits = jax.random.split(jax.random.key(seed), 3)
    return {
        "amps": draw_amps(jax.random.fold_in(splits[2], 71), 0),
        "conserve": draw_conserve(jax.random.fold_in(splits[2], 71), 0),
    }


def reference(amps, conserve):
    count_i = amps.shape[0]
    count_j = amps.shape[1]
    scale = 1.0 / (count_i * count_j * OP * V)
    rows_index = jnp.arange(count_i, dtype=jnp.int32)[:, None]
    cols_index = jnp.arange(count_j, dtype=jnp.int32)[None, :]

    def one_block(block):
        own = amps[:, :, block]
        pick = conserve[:, :, block]
        other = amps[rows_index, cols_index, pick]
        exchange = jnp.swapaxes(other, -1, -2)
        conj_mix = (2.0 * own.astype(jnp.float32) - exchange.astype(jnp.float32)).astype(jnp.bfloat16)
        total = jnp.einsum("rsoxc,rsoyc->xy", own.astype(jnp.float32), conj_mix.astype(jnp.float32), precision=lax.Precision.HIGHEST)
        return total * scale

    return lax.map(one_block, jnp.arange(KA, dtype=jnp.int32))
```

```python
import functools
import jax
import jax.numpy as jnp
from jax import lax
from jax.experimental import pallas as pl
from jax.experimental.pallas import tpu as pltpu
from jax.sharding import Mesh, PartitionSpec as P

FINE = ("x_hi", "y", "x_lo", "z", "core")
SIZES = (2, 4, 2, 8, 2)
GROUPS, WIDE, TILES, UNIT = 50, 3, 160, 40


def position(x, y, z, core):
    x, y, z, core = x % 4, y % 4, z % 8, core % 2
    return (((x // 2 * 4 + y) * 2 + x % 2) * 8 + z) * 2 + core


def pairs(move):
    found = []
    for x in range(4):
        for y in range(4):
            for z in range(8):
                for core in range(2):
                    dx, dy, dz, dc = move(x, y, z, core)
                    found.append((position(x, y, z, core), position(x + dx, y + dy, z + dz, core + dc)))
    return found


def send(value, move):
    return lax.ppermute(value, FINE, pairs(move))


def density_kernel(table, amps, keep, give, blocks, acc, tiles, in_sems, out_sems):
    count, orbitals, size = amps.shape[0], amps.shape[1], amps.shape[2]
    x = lax.axis_index("x_hi") * 2 + lax.axis_index("x_lo")
    y = lax.axis_index("y")
    core = lax.axis_index("core")

    def fetch(b):
        return pltpu.make_async_copy(amps.at[b], blocks.at[b], in_sems.at[b])

    for i in range(count):
        partner = table[i]

        @pl.when(partner >= i)
        def _():
            fetch(i).start()

        @pl.when(partner > i)
        def _():
            fetch(partner).start()

    lane = lax.broadcasted_iota(jnp.int32, (8, 128), 1)

    def step(i, carry):
        partner = table[i]

        @pl.when(partner >= i)
        def _():
            fetch(i).wait()

        @pl.when(partner > i)
        def _():
            fetch(partner).wait()

        total = None
        for o in range(orbitals):
            own = blocks[i, o]
            mix = (2.0 * own.T.astype(jnp.float32) - blocks[partner, o].astype(jnp.float32)).astype(jnp.bfloat16)
            part = jnp.dot(own, mix, preferred_element_type=jnp.float32)
            total = part if total is None else total + part
        acc[:, :size] = total

        slot = lax.rem(i, 2)

        def leave(half, low, target, k, j):
            return pltpu.make_async_copy(
                tiles.at[slot, half * 2 + low], target.at[k, j], out_sems.at[slot, half * 2 + low]
            )

        @pl.when(i >= 2)
        def _():
            for half in range(2):
                for low in range(2):
                    leave(half, low, keep, 0, 0).wait()

        for t in range(GROUPS * WIDE):
            g, l = divmod(t, WIDE)
            tiles[slot, t // UNIT, t % UNIT] = acc[8 * g : 8 * g + 8, 128 * l : 128 * l + 128]
        for n in range(7):
            t = GROUPS * WIDE + n
            tile = jnp.zeros((8, 128), jnp.float32)
            for k in range(min(8, GROUPS - 8 * n)):
                g = 8 * n + k
                piece = acc[8 * g : 8 * g + 8, 128 * WIDE : 128 * WIDE + 128]
                if k:
                    piece = pltpu.roll(piece, 16 * k, 1)
                tile = jnp.where((lane >= 16 * k) & (lane < 16 * k + 16), piece, tile)
            tiles[slot, t // UNIT, t % UNIT] = tile
        for t in range(GROUPS * WIDE + 7, TILES):
            tiles[slot, t // UNIT, t % UNIT] = jnp.zeros((8, 128), jnp.float32)

        high, dy = i // 4, lax.rem(i % 4 - y + 4, 4)
        for half in range(2):
            for low in range(2):
                dx = lax.rem(high * 2 + low - x + 4, 4)
                k, j = (dy, dx) if half == 0 else (dx, dy)

                @pl.when(core == half)
                def _():
                    leave(half, low, keep, k, j).start()

                @pl.when(core != half)
                def _():
                    leave(half, low, give, k, j).start()

        return carry

    lax.fori_loop(0, count, step, 0)
    for slot in range(2):
        for u in range(4):
            pltpu.make_async_copy(tiles.at[slot, u], keep.at[0, 0], out_sems.at[slot, u]).wait()


def densities(table, amps):
    count, orbitals, size, _ = amps.shape
    out = jax.ShapeDtypeStruct((4, 4, UNIT, 8, 128), jnp.float32)
    return pl.pallas_call(
        density_kernel,
        out_shape=(out, out),
        in_specs=[pl.BlockSpec(memory_space=pltpu.SMEM), pl.BlockSpec(memory_space=pl.ANY)],
        out_specs=(pl.BlockSpec(memory_space=pl.ANY), pl.BlockSpec(memory_space=pl.ANY)),
        scratch_shapes=[
            pltpu.VMEM(amps.shape, jnp.bfloat16),
            pltpu.VMEM((size, 512), jnp.float32),
            pltpu.VMEM((2, 4, UNIT, 8, 128), jnp.float32),
            pltpu.SemaphoreType.DMA((count,)),
            pltpu.SemaphoreType.DMA((2, 4)),
        ],
        compiler_params=pltpu.CompilerParams(vmem_limit_bytes=40 << 20),
        cost_estimate=pl.CostEstimate(flops=8 << 30, bytes_accessed=20 << 20, transcendentals=0),
        name="densities",
    )(table, amps)


def layout_kernel(scale, mine, beside, other, other_beside, out, whole, sems):
    low, core = lax.axis_index("x_lo"), lax.axis_index("core")
    copies = [
        pltpu.make_async_copy(ref, whole.at[pl.ds(u * UNIT, UNIT)], sems.at[n])
        for n, (ref, u) in enumerate(
            (
                (mine, core * 2 + low),
                (beside, core * 2 + 1 - low),
                (other, (1 - core) * 2 + low),
                (other_beside, (1 - core) * 2 + 1 - low),
            )
        )
    ]
    for copy in copies:
        copy.start()
    for copy in copies:
        copy.wait()
    for t in range(GROUPS * WIDE):
        g, l = divmod(t, WIDE)
        out[0, 8 * g : 8 * g + 8, 128 * l : 128 * l + 128] = whole[t] * scale
    for g in range(GROUPS):
        n, k = divmod(g, 8)
        tile = whole[GROUPS * WIDE + n] * scale
        if k:
            tile = pltpu.roll(tile, 128 - 16 * k, 1)
        out[0, 8 * g : 8 * g + 8, 128 * WIDE : 128 * WIDE + 16] = tile[:, :16]


def lay_out(scale, size, *units):
    return pl.pallas_call(
        functools.partial(layout_kernel, scale),
        out_shape=jax.ShapeDtypeStruct((1, size, size), jnp.float32),
        in_specs=[pl.BlockSpec(memory_space=pl.ANY)] * 4,
        out_specs=pl.BlockSpec(memory_space=pltpu.VMEM),
        scratch_shapes=[pltpu.VMEM((TILES, 8, 128), jnp.float32), pltpu.SemaphoreType.DMA((4,))],
        compiler_params=pltpu.CompilerParams(vmem_limit_bytes=8 << 20),
        name="lay_out",
    )(*units)


def on_device(amps, conserve):
    scale = 1.0 / (8 * 32 * amps.shape[3] * amps.shape[4])
    keep, give = densities(conserve[0, 0], amps[0, 0])

    got = send(give, lambda x, y, z, core: (0, 0, 0, 1))
    first = [keep[k] + got[k] for k in range(4)]
    came = [
        send(first[k], lambda x, y, z, core, k=k: (0, k, 0, 0) if core == 0 else (k, 0, 0, 0)) for k in (1, 2, 3)
    ]
    second = [first[0][j] + came[0][j] + came[1][j] + came[2][j] for j in range(4)]
    came = [
        send(second[j], lambda x, y, z, core, j=j: (j, 0, 0, 0) if core == 0 else (0, j, 0, 0)) for j in (1, 2, 3)
    ]
    third = second[0] + came[0] + came[1] + came[2]
    parts = lax.all_to_all(third.reshape(8, UNIT // 8, 8, 128), "z", 0, 0, tiled=True)
    eighth = jnp.sum(parts, axis=0, keepdims=True)
    mine = lax.all_to_all(jnp.broadcast_to(eighth, parts.shape), "z", 0, 0, tiled=True).reshape(UNIT, 8, 128)
    beside = send(mine, lambda x, y, z, core: (1 - 2 * (x % 2), 0, 0, 0))
    other = send(mine, lambda x, y, z, core: (0, 0, 0, 1))
    other_beside = send(beside, lambda x, y, z, core: (0, 0, 0, 1))
    return lay_out(scale, amps.shape[4], mine, beside, other, other_beside)


def solution(mesh):
    fine = Mesh(mesh.devices.reshape(SIZES), FINE)
    ki, kj = ("x_hi", "y"), ("x_lo", "z", "core")
    return jax.shard_map(
        on_device,
        mesh=fine,
        in_specs=(P(ki, kj, None, None, None, None), P(ki, kj, None)),
        out_specs=P(ki, None, None),
        check_vma=False,
    )
```

```python
import functools
import jax
import jax.numpy as jnp
from jax import lax
from jax.experimental import pallas as pl
from jax.experimental.pallas import tpu as pltpu
from jax.sharding import Mesh, PartitionSpec as P

FINE = ("x_hi", "y", "x_lo", "z", "core")
SIZES = (2, 4, 2, 8, 2)
GROUPS, WIDE, TILES, UNIT = 50, 3, 160, 40


def position(x, y, z, core):
    x, y, z, core = x % 4, y % 4, z % 8, core % 2
    return (((x // 2 * 4 + y) * 2 + x % 2) * 8 + z) * 2 + core


def pairs(move):
    found = []
    for x in range(4):
        for y in range(4):
            for z in range(8):
                for core in range(2):
                    dx, dy, dz, dc = move(x, y, z, core)
                    found.append((position(x, y, z, core), position(x + dx, y + dy, z + dz, core + dc)))
    return found


def send(value, move):
    return lax.ppermute(value, FINE, pairs(move))


def across(x, y, z, core):
    return 0, 0, 0, 1


def around(step, turn, x, y, z, core):
    return (0, (y ^ step) - y, 0, 0) if core == turn else ((x ^ step) - x, 0, 0, 0)


def block_of(place):
    run, y = place // 4, place % 4
    return (y // 2 ^ run) * 4 + y


def place_of(block):
    y = block % 4
    return (block // 4 ^ y // 2) * 4 + y


def density_kernel(run, table, amps, blocks, keep, give, acc, in_sems):
    count, orbitals, size = blocks.shape[0], blocks.shape[1], blocks.shape[2]
    x_low = lax.axis_index("x_lo")
    x = lax.axis_index("x_hi") * 2 + x_low
    y = lax.axis_index("y")
    core = lax.axis_index("core")

    def arrivals(place, o, act):
        block = block_of(place)
        partner = table[block]
        other_place = place_of(partner)

        @pl.when(other_place >= place)
        def _():
            act(pltpu.make_async_copy(amps.at[block], blocks.at[block], in_sems.at[block]))

        @pl.when(other_place > place)
        def _():
            act(pltpu.make_async_copy(amps.at[partner], blocks.at[partner], in_sems.at[partner]))

    if run == 0:
        for place in range(count):
            arrivals(place, slice(None), lambda copy: copy.start())

    lane = lax.broadcasted_iota(jnp.int32, (8, 128), 1)

    def tile_of(t):
        if t < GROUPS * WIDE:
            g, l = divmod(t, WIDE)
            return acc[8 * g : 8 * g + 8, 128 * l : 128 * l + 128]
        tile = jnp.zeros((8, 128), jnp.float32)
        first = 8 * (t - GROUPS * WIDE)
        for k in range(max(0, min(8, GROUPS - first))):
            g = first + k
            piece = acc[8 * g : 8 * g + 8, 128 * WIDE : 128 * WIDE + 128]
            if k:
                piece = pltpu.roll(piece, 16 * k, 1)
            tile = jnp.where((lane >= 16 * k) & (lane < 16 * k + 16), piece, tile)
        return tile

    def step(i, carry):
        place = run * 4 + i
        block = block_of(place)
        partner = table[block]
        total = None
        for o in range(orbitals):
            if run == 0 and o == 0:
                arrivals(place, slice(None), lambda copy: copy.wait())
            own = blocks[block, o]
            turned = own.T
            mix = turned + turned - blocks[partner, o]
            part = jnp.dot(own, mix, preferred_element_type=jnp.float32)
            total = part if total is None else total + part
        acc[:, :size] = total

        high, dy = block // 4, i ^ y
        for half in range(2):
            for target, here in ((keep, core == half), (give, core != half)):

                @pl.when(here)
                def _():
                    for low in range(2):
                        u, dx = half * 2 + low, (high * 2 + low) ^ x
                        k, j = (dy, low ^ x_low) if half == 0 else (dx, dy & 1)
                        for n in range(UNIT):
                            target[k, j, n] = tile_of(u * UNIT + n)

        return carry

    lax.fori_loop(0, 4, step, 0)
    if run == 0:
        for place in range(4, count):
            arrivals(place, slice(None), lambda copy: copy.wait())


def densities(run, table, amps, blocks=None):
    shape = amps.shape
    half = pltpu.VMEM((4, 2, UNIT, 8, 128), jnp.float32)
    in_vmem = pl.BlockSpec(memory_space=pltpu.VMEM)
    params = dict(
        compiler_params=pltpu.CompilerParams(vmem_limit_bytes=12 << 20),
        cost_estimate=pl.CostEstimate(flops=4 << 30, bytes_accessed=13 << 20, transcendentals=0),
        name="densities",
    )
    acc = pltpu.VMEM((shape[2], 512), jnp.float32)
    if run == 0:
        return pl.pallas_call(
            functools.partial(density_kernel, 0),
            out_shape=(pltpu.VMEM(shape, jnp.bfloat16), half, half),
            in_specs=[pl.BlockSpec(memory_space=pltpu.SMEM), pl.BlockSpec(memory_space=pltpu.HBM)],
            out_specs=(in_vmem,) * 3,
            scratch_shapes=[acc, pltpu.SemaphoreType.DMA(shape[:1])],
            **params,
        )(table, pltpu.with_memory_space_constraint(amps, pltpu.HBM))

    def later(table, blocks, keep, give, acc):
        density_kernel(run, table, None, blocks, keep, give, acc, None)

    return pl.pallas_call(
        later,
        out_shape=(half, half),
        in_specs=[pl.BlockSpec(memory_space=pltpu.SMEM), in_vmem],
        out_specs=(in_vmem,) * 2,
        scratch_shapes=[acc],
        **params,
    )(table, pltpu.with_memory_space_constraint(blocks, pltpu.VMEM))


def layout_kernel(scale, mine, beside, other, other_beside, out, whole):
    low, core = lax.axis_index("x_lo"), lax.axis_index("core")
    for ref, u in (
        (mine, core * 2 + low),
        (beside, core * 2 + 1 - low),
        (other, (1 - core) * 2 + low),
        (other_beside, (1 - core) * 2 + 1 - low),
    ):
        whole[pl.ds(u * UNIT, UNIT)] = ref[...] * scale
    for t in range(GROUPS * WIDE):
        g, l = divmod(t, WIDE)
        out[0, 8 * g : 8 * g + 8, 128 * l : 128 * l + 128] = whole[t]
    for g in range(GROUPS):
        n, k = divmod(g, 8)
        tile = whole[GROUPS * WIDE + n]
        if k:
            tile = pltpu.roll(tile, 128 - 16 * k, 1)
        out[0, 8 * g : 8 * g + 8, 128 * WIDE : 128 * WIDE + 16] = tile[:, :16]


def lay_out(scale, size, *units):
    return pl.pallas_call(
        functools.partial(layout_kernel, scale),
        out_shape=jax.ShapeDtypeStruct((1, size, size), jnp.float32),
        in_specs=[pl.BlockSpec(memory_space=pltpu.VMEM)] * 4,
        out_specs=pl.BlockSpec(memory_space=pltpu.VMEM),
        scratch_shapes=[pltpu.VMEM((TILES, 8, 128), jnp.float32)],
        compiler_params=pltpu.CompilerParams(vmem_limit_bytes=8 << 20),
        name="lay_out",
    )(*(pltpu.with_memory_space_constraint(unit, pltpu.VMEM) for unit in units))


def on_device(amps, conserve):
    scale = 1.0 / (8 * 32 * amps.shape[3] * amps.shape[4])
    table, own = conserve[0, 0], amps[0, 0]
    blocks, keep, give = densities(0, table, own)
    runs = [(keep, send(give, across)), None]
    keep, give = densities(1, table, own, blocks)
    runs[1] = (keep, send(give, across))

    sums = []
    for keep, got in runs:
        first = [keep[k] + got[k] for k in range(4)]
        came = [send(first[k], functools.partial(around, k, 0)) for k in (1, 2, 3)]
        sums.append(first[0] + came[0] + came[1] + came[2])
    swapped = (lax.axis_index("y") >> 1) != lax.axis_index("x_hi")
    second = [jnp.where(swapped, sums[1 - j // 2][j % 2], sums[j // 2][j % 2]) for j in range(4)]
    came = [send(second[j], functools.partial(around, j, 1)) for j in (1, 2, 3)]
    third = second[0] + came[0] + came[1] + came[2]
    parts = lax.all_to_all(third.reshape(8, UNIT // 8, 8, 128), "z", 0, 0, tiled=True)
    eighth = jnp.sum(parts, axis=0, keepdims=True)
    mine = lax.all_to_all(jnp.broadcast_to(eighth, parts.shape), "z", 0, 0, tiled=True).reshape(UNIT, 8, 128)
    beside = send(mine, lambda x, y, z, core: (1 - 2 * (x % 2), 0, 0, 0))
    other = send(mine, across)
    other_beside = send(beside, across)
    return lay_out(scale, amps.shape[4], mine, beside, other, other_beside)


def solution(mesh):
    fine = Mesh(mesh.devices.reshape(SIZES), FINE)
    ki, kj = ("x_hi", "y"), ("x_lo", "z", "core")
    return jax.shard_map(
        on_device,
        mesh=fine,
        in_specs=(P(ki, kj, None, None, None, None), P(ki, kj, None)),
        out_specs=P(ki, None, None),
        check_vma=False,
    )
```

```python
import functools
import jax
import jax.numpy as jnp
from jax import lax
from jax.experimental import pallas as pl
from jax.experimental.pallas import tpu as pltpu
from jax.sharding import Mesh, PartitionSpec as P

FINE = ("x_hi", "y", "x_lo", "z", "core")
SIZES = (2, 4, 2, 8, 2)
HALF_GROUPS, WIDE, UNIT, PIECE = 25, 3, 40, 10
FULL = HALF_GROUPS * WIDE


def position(x, y, z, core):
    x, y, z, core = x % 4, y % 4, z % 8, core % 2
    return (((x // 2 * 4 + y) * 2 + x % 2) * 8 + z) * 2 + core


def pairs(move):
    found = []
    for x in range(4):
        for y in range(4):
            for z in range(8):
                for core in range(2):
                    dx, dy, dz, dc = move(x, y, z, core)
                    found.append((position(x, y, z, core), position(x + dx, y + dy, z + dz, core + dc)))
    return found


def send(value, move):
    return lax.ppermute(value, FINE, pairs(move))


def across(x, y, z, core):
    return 0, 0, 0, 1


def around(step, turn, x, y, z, core):
    return (0, (y ^ step) - y, 0, 0) if core == turn else ((x ^ step) - x, 0, 0, 0)


def along(step, x, y, z, core):
    return 0, 0, (z ^ step) - z, 0


def block_of(place):
    run, y = place // 4, place % 4
    return (y // 2 ^ run) * 4 + y


def place_of(block):
    y = block % 4
    return (block // 4 ^ y // 2) * 4 + y


def density_kernel(run, table, amps, blocks, keep, give, acc, in_sems):
    count, orbitals, size = blocks.shape[0], blocks.shape[1], blocks.shape[2]
    x_low = lax.axis_index("x_lo")
    x = lax.axis_index("x_hi") * 2 + x_low
    y = lax.axis_index("y")
    core = lax.axis_index("core")
    starts = [(lax.axis_index("z") // 2 ^ q) * PIECE for q in range(4)]

    def arrivals(place, o, act):
        block = block_of(place)
        partner = table[block]
        other_place = place_of(partner)

        @pl.when(other_place >= place)
        def _():
            act(pltpu.make_async_copy(amps.at[block], blocks.at[block], in_sems.at[block]))

        @pl.when(other_place > place)
        def _():
            act(pltpu.make_async_copy(amps.at[partner], blocks.at[partner], in_sems.at[partner]))

    if run == 0:
        for place in range(count):
            arrivals(place, slice(None), lambda copy: copy.start())

    lane = lax.broadcasted_iota(jnp.int32, (8, 128), 1)

    def tile_of(acc, half, m):
        if m == UNIT * 2 - 1:
            return jnp.zeros((8, 128), jnp.float32)

        def read(g, l):
            row = pl.multiple_of(half * (8 * HALF_GROUPS) + 8 * g, 8)
            return acc[pl.ds(row, 8), 128 * l : 128 * l + 128]

        if m < FULL:
            return read(*divmod(m, WIDE))
        first = 8 * (m - FULL)
        tile = read(first, WIDE)
        for k in range(1, min(8, HALF_GROUPS - first)):
            tile = jnp.where(lane < 16 * k, tile, pltpu.roll(read(first + k, WIDE), 16 * k, 1))
        return tile

    def step(i, carry):
        place = run * 4 + i
        block = block_of(place)
        partner = table[block]
        total = None
        for o in range(orbitals):
            if run == 0 and o == 0:
                arrivals(place, slice(None), lambda copy: copy.wait())
            own = blocks[block, o]
            turned = own.T
            mix = turned + turned - blocks[partner, o]
            part = jnp.dot(own, mix, preferred_element_type=jnp.float32)
            total = part if total is None else total + part
        acc[:, :size] = total

        high, dy = block // 4, i ^ y
        for target, half in ((keep, core), (give, 1 - core)):
            for low in range(2):
                dx = (high * 2 + low) ^ x
                k = jnp.where(half == 0, dy, dx)
                j = jnp.where(half == 0, low ^ x_low, dy & 1)
                for n in range(UNIT):
                    target[k, j, starts[n // PIECE] + n % PIECE] = tile_of(acc, half, low * UNIT + n)

        return carry

    lax.fori_loop(0, 4, step, 0)
    if run == 0:
        for place in range(4, count):
            arrivals(place, slice(None), lambda copy: copy.wait())


def densities(run, table, amps, blocks=None):
    shape = amps.shape
    half = pltpu.VMEM((4, 2, UNIT, 8, 128), jnp.float32)
    in_vmem = pl.BlockSpec(memory_space=pltpu.VMEM)
    params = dict(
        compiler_params=pltpu.CompilerParams(vmem_limit_bytes=12 << 20),
        cost_estimate=pl.CostEstimate(flops=4 << 30, bytes_accessed=13 << 20, transcendentals=0),
        name="densities",
    )
    acc = pltpu.VMEM((shape[2], 512), jnp.float32)
    if run == 0:
        return pl.pallas_call(
            functools.partial(density_kernel, 0),
            out_shape=(pltpu.VMEM(shape, jnp.bfloat16), half, half),
            in_specs=[pl.BlockSpec(memory_space=pltpu.SMEM), pl.BlockSpec(memory_space=pltpu.HBM)],
            out_specs=(in_vmem,) * 3,
            scratch_shapes=[acc, pltpu.SemaphoreType.DMA(shape[:1])],
            **params,
        )(table, pltpu.with_memory_space_constraint(amps, pltpu.HBM))

    def later(table, blocks, keep, give, acc):
        density_kernel(run, table, None, blocks, keep, give, acc, None)

    return pl.pallas_call(
        later,
        out_shape=(half, half),
        in_specs=[pl.BlockSpec(memory_space=pltpu.SMEM), in_vmem],
        out_specs=(in_vmem,) * 2,
        scratch_shapes=[acc],
        **params,
    )(table, pltpu.with_memory_space_constraint(blocks, pltpu.VMEM))


def combine(body, outs, *arrays):
    in_vmem = pl.BlockSpec(memory_space=pltpu.VMEM)
    return pl.pallas_call(
        body,
        out_shape=tuple(pltpu.VMEM(shape, jnp.float32) for shape in outs),
        in_specs=[in_vmem] * len(arrays),
        out_specs=(in_vmem,) * len(outs),
        compiler_params=pltpu.CompilerParams(vmem_limit_bytes=4 << 20),
        name=body.__name__,
    )(*(pltpu.with_memory_space_constraint(array, pltpu.VMEM) for array in arrays))


def add_halves(keep, got, *sums):
    for k, out in enumerate(sums):
        out[...] = keep[k] + got[k]


def add_ring(*refs):
    arrived, sums = refs[:8], refs[8:]
    swapped = (lax.axis_index("y") >> 1) ^ lax.axis_index("x_hi")
    for turn in range(2):

        @pl.when(swapped == turn)
        def _():
            for run in range(2):
                a, b, c, d = arrived[4 * run : 4 * run + 4]
                for low in range(2):
                    sums[2 * (run ^ turn) + low][...] = (a[low] + b[low]) + (c[low] + d[low])


def add_last(*refs):
    a, b, c, d = refs[:4]
    for r, out in enumerate(refs[4:]):
        part = slice(r * PIECE, (r + 1) * PIECE)
        out[...] = (a[part] + b[part]) + (c[part] + d[part])


def layout_kernel(scale, mine, beside, other, other_beside, out, whole):
    low, core = lax.axis_index("x_lo"), lax.axis_index("core")
    away = lax.axis_index("z") // 2
    for ref, u in (
        (mine, core * 2 + low),
        (beside, core * 2 + 1 - low),
        (other, (1 - core) * 2 + low),
        (other_beside, (1 - core) * 2 + 1 - low),
    ):
        for r in range(4):
            whole[pl.ds(u * UNIT + (away ^ r) * PIECE, PIECE)] = ref[r * PIECE : (r + 1) * PIECE] * scale
    for half in range(2):
        for m in range(FULL):
            g, l = divmod(m, WIDE)
            row = 8 * (half * HALF_GROUPS + g)
            out[0, row : row + 8, 128 * l : 128 * l + 128] = whole[half * 2 * UNIT + m]
        for g in range(HALF_GROUPS):
            n, k = divmod(g, 8)
            tile = whole[half * 2 * UNIT + FULL + n]
            if k:
                tile = pltpu.roll(tile, 128 - 16 * k, 1)
            row = 8 * (half * HALF_GROUPS + g)
            out[0, row : row + 8, 128 * WIDE : 128 * WIDE + 16] = tile[:, :16]


def lay_out(scale, size, *units):
    return pl.pallas_call(
        functools.partial(layout_kernel, scale),
        out_shape=jax.ShapeDtypeStruct((1, size, size), jnp.float32),
        in_specs=[pl.BlockSpec(memory_space=pltpu.VMEM)] * 4,
        out_specs=pl.BlockSpec(memory_space=pltpu.VMEM),
        scratch_shapes=[pltpu.VMEM((4 * UNIT, 8, 128), jnp.float32)],
        compiler_params=pltpu.CompilerParams(vmem_limit_bytes=8 << 20),
        name="lay_out",
    )(*(pltpu.with_memory_space_constraint(unit, pltpu.VMEM) for unit in units))


def on_device(amps, conserve):
    scale = 1.0 / (8 * 32 * amps.shape[3] * amps.shape[4])
    table, own = conserve[0, 0], amps[0, 0]
    blocks, keep, give = densities(0, table, own)
    runs = [(keep, send(give, across)), None]
    keep, give = densities(1, table, own, blocks)
    runs[1] = (keep, send(give, across))

    unit, piece = (UNIT, 8, 128), (PIECE, 8, 128)
    arrived = []
    for keep, got in runs:
        first = combine(add_halves, [(2, *unit)] * 4, keep, got)
        arrived += [first[0]] + [send(first[k], functools.partial(around, k, 0)) for k in (1, 2, 3)]
    second = combine(add_ring, [unit] * 4, *arrived)
    came = [send(second[j], functools.partial(around, j, 1)) for j in (1, 2, 3)]
    third = combine(add_last, [piece] * 4, second[0], *came)
    came = [send(third[r], functools.partial(along, 2 * r)) for r in (1, 2, 3)]
    fourth = (third[0] + came[0]) + (came[1] + came[2])
    fifth = fourth + send(fourth, functools.partial(along, 1))
    mine = jnp.concatenate([fifth] + [send(fifth, functools.partial(along, 2 * r)) for r in (1, 2, 3)])
    beside = send(mine, lambda x, y, z, core: (1 - 2 * (x % 2), 0, 0, 0))
    other = send(mine, across)
    other_beside = send(beside, across)
    return lay_out(scale, amps.shape[4], mine, beside, other, other_beside)


def solution(mesh):
    fine = Mesh(mesh.devices.reshape(SIZES), FINE)
    ki, kj = ("x_hi", "y"), ("x_lo", "z", "core")
    return jax.shard_map(
        on_device,
        mesh=fine,
        in_specs=(P(ki, kj, None, None, None, None), P(ki, kj, None)),
        out_specs=P(ki, None, None),
        check_vma=False,
    )
```

```python
import functools
import jax
import jax.numpy as jnp
from jax import lax
from jax.experimental import pallas as pl
from jax.experimental.pallas import tpu as pltpu
from jax.sharding import Mesh, PartitionSpec as P

FINE = ("x_hi", "y", "x_lo", "z", "core")
SIZES = (2, 4, 2, 8, 2)
HALF_GROUPS, WIDE, UNIT = 25, 3, 40
FULL = HALF_GROUPS * WIDE


def position(x, y, z, core):
    x, y, z, core = x % 4, y % 4, z % 8, core % 2
    return (((x // 2 * 4 + y) * 2 + x % 2) * 8 + z) * 2 + core


def pairs(move):
    found = []
    for x in range(4):
        for y in range(4):
            for z in range(8):
                for core in range(2):
                    dx, dy, dz, dc = move(x, y, z, core)
                    found.append((position(x, y, z, core), position(x + dx, y + dy, z + dz, core + dc)))
    return found


def send(value, move):
    return lax.ppermute(value, FINE, pairs(move))


def across(x, y, z, core):
    return 0, 0, 0, 1


def around(step, turn, x, y, z, core):
    return (0, (y ^ step) - y, 0, 0) if core == turn else ((x ^ step) - x, 0, 0, 0)


def block_of(place):
    run, y = place // 4, place % 4
    return (y // 2 ^ run) * 4 + y


def place_of(block):
    y = block % 4
    return (block // 4 ^ y // 2) * 4 + y


def density_kernel(run, table, amps, blocks, keep, give, acc, in_sems):
    count, orbitals, size = blocks.shape[0], blocks.shape[1], blocks.shape[2]
    x_low = lax.axis_index("x_lo")
    x = lax.axis_index("x_hi") * 2 + x_low
    y = lax.axis_index("y")
    core = lax.axis_index("core")

    def arrivals(place, o, act):
        block = block_of(place)
        partner = table[block]
        other_place = place_of(partner)

        @pl.when(other_place >= place)
        def _():
            act(pltpu.make_async_copy(amps.at[block], blocks.at[block], in_sems.at[block]))

        @pl.when(other_place > place)
        def _():
            act(pltpu.make_async_copy(amps.at[partner], blocks.at[partner], in_sems.at[partner]))

    if run == 0:
        for place in range(count):
            arrivals(place, slice(None), lambda copy: copy.start())

    lane = lax.broadcasted_iota(jnp.int32, (8, 128), 1)

    def tile_of(acc, half, m):
        if m == UNIT * 2 - 1:
            return jnp.zeros((8, 128), jnp.float32)

        def read(g, l):
            row = pl.multiple_of(half * (8 * HALF_GROUPS) + 8 * g, 8)
            return acc[pl.ds(row, 8), 128 * l : 128 * l + 128]

        if m < FULL:
            return read(*divmod(m, WIDE))
        first = 8 * (m - FULL)
        tile = read(first, WIDE)
        for k in range(1, min(8, HALF_GROUPS - first)):
            tile = jnp.where(lane < 16 * k, tile, pltpu.roll(read(first + k, WIDE), 16 * k, 1))
        return tile

    def step(i, carry):
        place = run * 4 + i
        block = block_of(place)
        partner = table[block]
        total = None
        for o in range(orbitals):
            if run == 0 and o == 0:
                arrivals(place, slice(None), lambda copy: copy.wait())
            own = blocks[block, o]
            turned = own.T
            mix = turned + turned - blocks[partner, o]
            part = jnp.dot(own, mix, preferred_element_type=jnp.float32)
            total = part if total is None else total + part
        acc[:, :size] = total

        high, dy = block // 4, i ^ y
        for target, half in ((keep, core), (give, 1 - core)):
            for low in range(2):
                dx = (high * 2 + low) ^ x
                k = jnp.where(half == 0, dy, dx)
                j = jnp.where(half == 0, low ^ x_low, dy & 1)
                for n in range(UNIT):
                    target[k, j, n] = tile_of(acc, half, low * UNIT + n)

        return carry

    lax.fori_loop(0, 4, step, 0)
    if run == 0:
        for place in range(4, count):
            arrivals(place, slice(None), lambda copy: copy.wait())


def densities(run, table, amps, blocks=None):
    shape = amps.shape
    half = pltpu.VMEM((4, 2, UNIT, 8, 128), jnp.float32)
    in_vmem = pl.BlockSpec(memory_space=pltpu.VMEM)
    params = dict(
        compiler_params=pltpu.CompilerParams(vmem_limit_bytes=12 << 20),
        cost_estimate=pl.CostEstimate(flops=4 << 30, bytes_accessed=13 << 20, transcendentals=0),
        name="densities",
    )
    acc = pltpu.VMEM((shape[2], 512), jnp.float32)
    if run == 0:
        return pl.pallas_call(
            functools.partial(density_kernel, 0),
            out_shape=(pltpu.VMEM(shape, jnp.bfloat16), half, half),
            in_specs=[pl.BlockSpec(memory_space=pltpu.SMEM), pl.BlockSpec(memory_space=pltpu.HBM)],
            out_specs=(in_vmem,) * 3,
            scratch_shapes=[acc, pltpu.SemaphoreType.DMA(shape[:1])],
            **params,
        )(table, pltpu.with_memory_space_constraint(amps, pltpu.HBM))

    def later(table, blocks, keep, give, acc):
        density_kernel(run, table, None, blocks, keep, give, acc, None)

    return pl.pallas_call(
        later,
        out_shape=(half, half),
        in_specs=[pl.BlockSpec(memory_space=pltpu.SMEM), in_vmem],
        out_specs=(in_vmem,) * 2,
        scratch_shapes=[acc],
        **params,
    )(table, pltpu.with_memory_space_constraint(blocks, pltpu.VMEM))


def combine(body, outs, *arrays):
    in_vmem = pl.BlockSpec(memory_space=pltpu.VMEM)
    return pl.pallas_call(
        body,
        out_shape=tuple(pltpu.VMEM(shape, jnp.float32) for shape in outs),
        in_specs=[in_vmem] * len(arrays),
        out_specs=(in_vmem,) * len(outs),
        compiler_params=pltpu.CompilerParams(vmem_limit_bytes=4 << 20),
        name=body.__name__,
    )(*(pltpu.with_memory_space_constraint(array, pltpu.VMEM) for array in arrays))


def add_halves(keep, got, send_a, keep_a, send_b, keep_b):
    for low, out, distances in ((0, send_a, (1, 2)), (0, keep_a, (0, 3)), (1, send_b, (3, 2)), (1, keep_b, (0, 1))):
        for n, k in enumerate(distances):
            out[n] = keep[k, low] + got[k, low]


def add_first(keep_a, got_a, keep_b, got_b, own_a, send_a, own_b, send_b):
    own_a[...] = keep_a[0] + got_a[0]
    send_a[...] = keep_a[1] + got_a[1]
    own_b[...] = keep_b[0] + got_b[0]
    send_b[...] = keep_b[1] + got_b[1]


def add_ring(*refs):
    arrived, sums = refs[:8], refs[8:]
    swapped = (lax.axis_index("y") >> 1) ^ lax.axis_index("x_hi")
    for turn in range(2):

        @pl.when(swapped == turn)
        def _():
            for run in range(2):
                for low in range(2):
                    own, got = arrived[4 * run + 2 * low : 4 * run + 2 * low + 2]
                    sums[2 * (run ^ turn) + low][...] = own[...] + got[...]


def layout_kernel(scale, mine, other, out, whole):
    core = lax.axis_index("core")
    whole[pl.ds(core * 2 * UNIT, 2 * UNIT)] = mine[...] * scale
    whole[pl.ds((1 - core) * 2 * UNIT, 2 * UNIT)] = other[...] * scale
    for half in range(2):
        for m in range(FULL):
            g, l = divmod(m, WIDE)
            row = 8 * (half * HALF_GROUPS + g)
            out[0, row : row + 8, 128 * l : 128 * l + 128] = whole[half * 2 * UNIT + m]
        for g in range(HALF_GROUPS):
            n, k = divmod(g, 8)
            tile = whole[half * 2 * UNIT + FULL + n]
            if k:
                tile = pltpu.roll(tile, 128 - 16 * k, 1)
            row = 8 * (half * HALF_GROUPS + g)
            out[0, row : row + 8, 128 * WIDE : 128 * WIDE + 16] = tile[:, :16]


def lay_out(scale, size, *units):
    return pl.pallas_call(
        functools.partial(layout_kernel, scale),
        out_shape=jax.ShapeDtypeStruct((1, size, size), jnp.float32),
        in_specs=[pl.BlockSpec(memory_space=pltpu.VMEM)] * 2,
        out_specs=pl.BlockSpec(memory_space=pltpu.VMEM),
        scratch_shapes=[pltpu.VMEM((4 * UNIT, 8, 128), jnp.float32)],
        compiler_params=pltpu.CompilerParams(vmem_limit_bytes=8 << 20),
        name="lay_out",
    )(*(pltpu.with_memory_space_constraint(unit, pltpu.VMEM) for unit in units))


def on_device(amps, conserve):
    scale = 1.0 / (8 * 32 * amps.shape[3] * amps.shape[4])
    table, own = conserve[0, 0], amps[0, 0]
    blocks, keep, give = densities(0, table, own)
    runs = [(keep, send(give, across)), None]
    keep, give = densities(1, table, own, blocks)
    runs[1] = (keep, send(give, across))

    unit = (UNIT, 8, 128)
    begun = []
    for keep, got in runs:
        send_a, keep_a, send_b, keep_b = combine(add_halves, [(2, *unit)] * 4, keep, got)
        begun.append((keep_a, send(send_a, functools.partial(around, 1, 0)), keep_b, send(send_b, functools.partial(around, 3, 0))))
    arrived = []
    for halves in begun:
        own_a, send_a, own_b, send_b = combine(add_first, [unit] * 4, *halves)
        arrived += [own_a, send(send_a, functools.partial(around, 3, 0)), own_b, send(send_b, functools.partial(around, 1, 0))]
    second = combine(add_ring, [unit] * 4, *arrived)
    came = [send(second[j], functools.partial(around, j, 1)) for j in (1, 2, 3)]
    third = (second[0] + came[0]) + (came[1] + came[2])
    parts = lax.all_to_all(third.reshape(8, UNIT // 8, 8, 128), "z", 0, 0, tiled=True)
    eighth = jnp.sum(parts, axis=0, keepdims=True)
    mine = lax.all_to_all(jnp.broadcast_to(eighth, (16, *parts.shape[1:])), ("x_lo", "z"), 0, 0, tiled=True)
    mine = mine.reshape(2 * UNIT, 8, 128)
    return lay_out(scale, amps.shape[4], mine, send(mine, across))


def solution(mesh):
    fine = Mesh(mesh.devices.reshape(SIZES), FINE)
    ki, kj = ("x_hi", "y"), ("x_lo", "z", "core")
    return jax.shard_map(
        on_device,
        mesh=fine,
        in_specs=(P(ki, kj, None, None, None, None), P(ki, kj, None)),
        out_specs=P(ki, None, None),
        check_vma=False,
    )
```

```python
import functools
import jax
import jax.numpy as jnp
from jax import lax
from jax.experimental import pallas as pl
from jax.experimental.pallas import tpu as pltpu
from jax.sharding import Mesh, PartitionSpec as P

FINE = ("x_hi", "y", "x_lo", "z", "core")
SIZES = (2, 4, 2, 8, 2)
HALF_GROUPS, WIDE, UNIT = 25, 3, 40
FULL = HALF_GROUPS * WIDE


def position(x, y, z, core):
    x, y, z, core = x % 4, y % 4, z % 8, core % 2
    return (((x // 2 * 4 + y) * 2 + x % 2) * 8 + z) * 2 + core


def pairs(move):
    found = []
    for x in range(4):
        for y in range(4):
            for z in range(8):
                for core in range(2):
                    dx, dy, dz, dc = move(x, y, z, core)
                    found.append((position(x, y, z, core), position(x + dx, y + dy, z + dz, core + dc)))
    return found


def send(value, move):
    return lax.ppermute(value, FINE, pairs(move))


def across(x, y, z, core):
    return 0, 0, 0, 1


def around(step, turn, x, y, z, core):
    return (0, (y ^ step) - y, 0, 0) if core == turn else ((x ^ step) - x, 0, 0, 0)


def add_block(blocks, acc, target, block, half, mix):
    x_low = lax.axis_index("x_lo")
    x, y = lax.axis_index("x_hi") * 2 + x_low, lax.axis_index("y")
    rows = pl.ds(pl.multiple_of(half * (8 * HALF_GROUPS - 8), 16), 8 * HALF_GROUPS + 8)
    size = blocks.shape[2]
    total = None
    for o in range(blocks.shape[1]):
        part = jnp.dot(blocks[block, o, rows, :], mix(o), preferred_element_type=jnp.float32)
        total = part if total is None else total + part
    acc[:, :size] = total

    lane = lax.broadcasted_iota(jnp.int32, (8, 128), 1)

    def read(g, l):
        return acc[pl.ds(pl.multiple_of(half * 8 + 8 * g, 8), 8), 128 * l : 128 * l + 128]

    def tile_of(m):
        if m == UNIT * 2 - 1:
            return jnp.zeros((8, 128), jnp.float32)
        if m < FULL:
            return read(*divmod(m, WIDE))
        first = 8 * (m - FULL)
        tile = read(first, WIDE)
        for k in range(1, min(8, HALF_GROUPS - first)):
            tile = jnp.where(lane < 16 * k, tile, pltpu.roll(read(first + k, WIDE), 16 * k, 1))
        return tile

    high, dy = block // 4, (block % 4) ^ y
    for low in range(2):
        dx = (high * 2 + low) ^ x
        k = jnp.where(half == 0, dy, dx)
        j = jnp.where(half == 0, dx, dy)
        for n in range(UNIT):
            target[k, j, n] = tile_of(low * UNIT + n)


def give_kernel(table_in, amps, blocks, mixes, give, acc, table, table_sem, sems):
    pltpu.make_async_copy(amps.at[0], blocks.at[0], sems.at[0]).start()
    copy = pltpu.make_async_copy(table_in, table, table_sem)
    copy.start()
    copy.wait()
    count, orbitals = blocks.shape[:2]
    half = 1 - lax.axis_index("core")

    def arrivals(block, act, own=True):
        partner = table[block]

        @pl.when((partner >= block) & own)
        def _():
            act(pltpu.make_async_copy(amps.at[block], blocks.at[block], sems.at[block]))

        @pl.when(partner > block)
        def _():
            act(pltpu.make_async_copy(amps.at[partner], blocks.at[partner], sems.at[partner]))

    for block in range(count):
        arrivals(block, lambda copy: copy.start(), block > 0)

    def step(pair, carry):
        first = pair * 2
        for block in (first, first + 1):
            arrivals(block, lambda copy: copy.wait())
        for block, own_acc in ((first, acc.at[0]), (first + 1, acc.at[1])):
            partner = table[block]

            def mix(o, block=block, partner=partner):
                turned = blocks[block, o].T
                value = turned + turned - blocks[partner, o]
                mixes[block, o] = value
                return value

            add_block(blocks, own_acc, give, block, half, mix)
        return carry

    lax.fori_loop(0, count // 2, step, 0)


def keep_kernel(blocks, mixes, keep, acc):
    half = lax.axis_index("core")

    def step(group, carry):
        for n in range(4):
            block = group * 4 + n
            add_block(blocks, acc.at[n % 2], keep, block, half, lambda o, block=block: mixes[block, o])
        return carry

    lax.fori_loop(0, blocks.shape[0] // 4, step, 0)


def kernel_params(name):
    return dict(
        compiler_params=pltpu.CompilerParams(vmem_limit_bytes=10 << 20),
        cost_estimate=pl.CostEstimate(flops=4 << 30, bytes_accessed=13 << 20, transcendentals=0),
        name=name,
    )


def give_half(table, amps):
    in_vmem = pl.BlockSpec(memory_space=pltpu.VMEM)
    whole = pltpu.VMEM(amps.shape, amps.dtype)
    return pl.pallas_call(
        give_kernel,
        out_shape=(whole, whole, pltpu.VMEM((4, 4, UNIT, 8, 128), jnp.float32)),
        in_specs=[pl.BlockSpec(memory_space=pltpu.HBM)] * 2,
        out_specs=(in_vmem,) * 3,
        scratch_shapes=[pltpu.VMEM((2, 8 * HALF_GROUPS + 8, 512), jnp.float32), pltpu.SMEM(table.shape, jnp.int32), pltpu.SemaphoreType.DMA, pltpu.SemaphoreType.DMA(amps.shape[:1])],
        **kernel_params("give_half"),
    )(*(pltpu.with_memory_space_constraint(array, pltpu.HBM) for array in (table, amps)))


def keep_half(blocks, mixes):
    in_vmem = pl.BlockSpec(memory_space=pltpu.VMEM)
    return pl.pallas_call(
        keep_kernel,
        out_shape=pltpu.VMEM((4, 4, UNIT, 8, 128), jnp.float32),
        in_specs=[in_vmem] * 2,
        out_specs=in_vmem,
        scratch_shapes=[pltpu.VMEM((2, 8 * HALF_GROUPS + 8, 512), jnp.float32)],
        **kernel_params("keep_half"),
    )(*(pltpu.with_memory_space_constraint(array, pltpu.VMEM) for array in (blocks, mixes)))


def combine(body, outs, *arrays):
    in_vmem = pl.BlockSpec(memory_space=pltpu.VMEM)
    return pl.pallas_call(
        body,
        out_shape=tuple(pltpu.VMEM(shape, jnp.float32) for shape in outs),
        in_specs=[in_vmem] * len(arrays),
        out_specs=(in_vmem,) * len(outs),
        compiler_params=pltpu.CompilerParams(vmem_limit_bytes=4 << 20),
        name=body.__name__,
    )(*(pltpu.with_memory_space_constraint(array, pltpu.VMEM) for array in arrays))


def add_halves(keep, got, send_a, keep_a, send_b, keep_b):
    for first, out, distances in ((0, send_a, (1, 2)), (0, keep_a, (0, 3)), (2, send_b, (3, 2)), (2, keep_b, (0, 1))):
        for n, k in enumerate(distances):
            for j in range(2):
                out[n, j] = keep[k, first + j] + got[k, first + j]


def add_first(keep_a, got_a, keep_b, got_b, own_a, send_a, own_b, send_b):
    own_a[...] = keep_a[0] + got_a[0]
    send_a[...] = keep_a[1] + got_a[1]
    own_b[...] = keep_b[0] + got_b[0]
    send_b[...] = keep_b[1] + got_b[1]


def add_second(own_a, got_a, own_b, got_b, *sums):
    for j in range(2):
        sums[j][...] = own_a[j] + got_a[j]
        sums[2 + j][...] = own_b[j] + got_b[j]


def layout_kernel(scale, mine, other, out, whole):
    core = lax.axis_index("core")
    whole[pl.ds(core * 2 * UNIT, 2 * UNIT)] = mine[...] * scale
    whole[pl.ds((1 - core) * 2 * UNIT, 2 * UNIT)] = other[...] * scale
    for half in range(2):
        for m in range(FULL):
            g, l = divmod(m, WIDE)
            row = 8 * (half * HALF_GROUPS + g)
            out[0, row : row + 8, 128 * l : 128 * l + 128] = whole[half * 2 * UNIT + m]
        for g in range(HALF_GROUPS):
            n, k = divmod(g, 8)
            tile = whole[half * 2 * UNIT + FULL + n]
            if k:
                tile = pltpu.roll(tile, 128 - 16 * k, 1)
            row = 8 * (half * HALF_GROUPS + g)
            out[0, row : row + 8, 128 * WIDE : 128 * WIDE + 16] = tile[:, :16]


def lay_out(scale, size, *units):
    return pl.pallas_call(
        functools.partial(layout_kernel, scale),
        out_shape=jax.ShapeDtypeStruct((1, size, size), jnp.float32),
        in_specs=[pl.BlockSpec(memory_space=pltpu.VMEM)] * 2,
        out_specs=pl.BlockSpec(memory_space=pltpu.VMEM),
        scratch_shapes=[pltpu.VMEM((4 * UNIT, 8, 128), jnp.float32)],
        compiler_params=pltpu.CompilerParams(vmem_limit_bytes=8 << 20),
        name="lay_out",
    )(*(pltpu.with_memory_space_constraint(unit, pltpu.VMEM) for unit in units))


def on_device(amps, conserve):
    scale = 1.0 / (8 * 32 * amps.shape[3] * amps.shape[4])
    table, own = conserve[0, 0], amps[0, 0]
    blocks, mixes, give = give_half(table, own)
    got = send(give, across)
    keep = keep_half(blocks, mixes)

    unit = (UNIT, 8, 128)
    send_a, keep_a, send_b, keep_b = combine(add_halves, [(2, 2, *unit)] * 4, keep, got)
    halves = keep_a, send(send_a, functools.partial(around, 1, 0)), keep_b, send(send_b, functools.partial(around, 3, 0))
    own_a, send_a, own_b, send_b = combine(add_first, [(2, *unit)] * 4, *halves)
    halves = own_a, send(send_a, functools.partial(around, 3, 0)), own_b, send(send_b, functools.partial(around, 1, 0))
    second = combine(add_second, [unit] * 4, *halves)
    came = [send(second[j], functools.partial(around, j, 1)) for j in (1, 2, 3)]
    third = (second[0] + came[0]) + (came[1] + came[2])
    parts = lax.all_to_all(third.reshape(8, UNIT // 8, 8, 128), "z", 0, 0, tiled=True)
    eighth = jnp.sum(parts, axis=0, keepdims=True)
    mine = lax.all_to_all(jnp.broadcast_to(eighth, (16, *parts.shape[1:])), ("x_lo", "z"), 0, 0, tiled=True)
    mine = mine.reshape(2 * UNIT, 8, 128)
    return lay_out(scale, amps.shape[4], mine, send(mine, across))


def solution(mesh):
    fine = Mesh(mesh.devices.reshape(SIZES), FINE)
    ki, kj = ("x_hi", "y"), ("x_lo", "z", "core")
    return jax.shard_map(
        on_device,
        mesh=fine,
        in_specs=(P(ki, kj, None, None, None, None), P(ki, kj, None)),
        out_specs=P(ki, None, None),
        check_vma=False,
    )
```

```python
import functools
import jax
import jax.numpy as jnp
from jax import lax
from jax.experimental import pallas as pl
from jax.experimental.pallas import tpu as pltpu
from jax.sharding import Mesh, PartitionSpec as P

FINE = ("x_hi", "y", "x_lo", "z", "core")
SIZES = (2, 4, 2, 8, 2)
HALF_GROUPS, WIDE, UNIT = 25, 3, 40
FULL = HALF_GROUPS * WIDE


def position(x, y, z, core):
    x, y, z, core = x % 4, y % 4, z % 8, core % 2
    return (((x // 2 * 4 + y) * 2 + x % 2) * 8 + z) * 2 + core


def pairs(move):
    found = []
    for x in range(4):
        for y in range(4):
            for z in range(8):
                for core in range(2):
                    dx, dy, dz, dc = move(x, y, z, core)
                    found.append((position(x, y, z, core), position(x + dx, y + dy, z + dz, core + dc)))
    return found


def send(value, move):
    return lax.ppermute(value, FINE, pairs(move))


def across(x, y, z, core):
    return 0, 0, 0, 1


def around(step, turn, x, y, z, core):
    return (0, (y ^ step) - y, 0, 0) if core == turn else ((x ^ step) - x, 0, 0, 0)


def block_of(place):
    run, y = place // 4, place % 4
    return (y // 2 ^ run) * 4 + y


def place_of(block):
    y = block % 4
    return (block // 4 ^ y // 2) * 4 + y


def add_block(blocks, acc, keep, give, block, partner, arrive=None):
    size = blocks.shape[2]
    x_low = lax.axis_index("x_lo")
    x, y = lax.axis_index("x_hi") * 2 + x_low, lax.axis_index("y")
    core = lax.axis_index("core")
    total = None
    for o in range(blocks.shape[1]):
        if arrive is not None:
            arrive(o)
        own = blocks[block, o]
        turned = own.T
        mix = turned + turned - blocks[partner, o]
        part = jnp.dot(own, mix, preferred_element_type=jnp.float32)
        total = part if total is None else total + part
    acc[:, :size] = total

    lane = lax.broadcasted_iota(jnp.int32, (8, 128), 1)

    def tile_of(half, m):
        if m == UNIT * 2 - 1:
            return jnp.zeros((8, 128), jnp.float32)

        def read(g, l):
            row = pl.multiple_of(half * (8 * HALF_GROUPS) + 8 * g, 8)
            return acc[pl.ds(row, 8), 128 * l : 128 * l + 128]

        if m < FULL:
            return read(*divmod(m, WIDE))
        first = 8 * (m - FULL)
        tile = read(first, WIDE)
        for k in range(1, min(8, HALF_GROUPS - first)):
            tile = jnp.where(lane < 16 * k, tile, pltpu.roll(read(first + k, WIDE), 16 * k, 1))
        return tile

    high, dy = block // 4, (block % 4) ^ y
    for target, half in ((keep, core), (give, 1 - core)):
        for low in range(2):
            dx = (high * 2 + low) ^ x
            k = jnp.where(half == 0, dy, dx)
            j = jnp.where(half == 0, low ^ x_low, dy & 1)
            for n in range(UNIT):
                target[k, j, n] = tile_of(half, low * UNIT + n)


def first_kernel(table_in, amps, blocks, keep, give, acc, table, table_sem, sems, early):
    count, orbitals = blocks.shape[:2]

    def fetch(block, o=None):
        if o is None:
            return pltpu.make_async_copy(amps.at[block], blocks.at[block], sems.at[block])
        return pltpu.make_async_copy(amps.at[block, o], blocks.at[block, o], early.at[block, o])

    def arrivals(place, act, o=None):
        block = block_of(place)
        partner = table[block]
        other_place = place_of(partner)

        @pl.when(other_place >= place)
        def _():
            act(fetch(block, o))

        @pl.when(other_place > place)
        def _():
            act(fetch(partner, o))

    fetch(0, 0).start()
    copy = pltpu.make_async_copy(table_in, table, table_sem)
    copy.start()
    copy.wait()
    partner = table[0]
    for o in range(orbitals):
        if o:
            fetch(0, o).start()

        @pl.when(partner > 0)
        def _():
            fetch(partner, o).start()

    for place in range(1, count):
        arrivals(place, lambda copy: copy.start())

    add_block(blocks, acc.at[0], keep, give, 0, partner, lambda o: arrivals(0, lambda copy: copy.wait(), o))

    def step(place, carry):
        arrivals(place, lambda copy: copy.wait())
        block = block_of(place)
        add_block(blocks, acc.at[1], keep, give, block, table[block])
        return carry

    lax.fori_loop(1, 4, step, 0)
    for place in range(4, count):
        arrivals(place, lambda copy: copy.wait())


def second_kernel(table, blocks, keep, give, acc):
    for i in range(4):
        block = block_of(4 + i)
        add_block(blocks, acc.at[i % 2], keep, give, block, table[block])


def densities(run, table, amps):
    half = pltpu.VMEM((4, 2, UNIT, 8, 128), jnp.float32)
    in_vmem = pl.BlockSpec(memory_space=pltpu.VMEM)
    acc = pltpu.VMEM((2, amps.shape[2], 512), jnp.float32)
    params = dict(
        compiler_params=pltpu.CompilerParams(vmem_limit_bytes=12 << 20),
        cost_estimate=pl.CostEstimate(flops=4 << 30, bytes_accessed=13 << 20, transcendentals=0),
        name="densities",
    )
    if run == 0:
        dma = pltpu.SemaphoreType.DMA
        return pl.pallas_call(
            first_kernel,
            out_shape=(pltpu.VMEM(amps.shape, amps.dtype), half, half),
            in_specs=[pl.BlockSpec(memory_space=pltpu.HBM)] * 2,
            out_specs=(in_vmem,) * 3,
            scratch_shapes=[acc, pltpu.SMEM(table.shape, table.dtype), dma, dma(amps.shape[:1]), dma(amps.shape[:2])],
            **params,
        )(*(pltpu.with_memory_space_constraint(array, pltpu.HBM) for array in (table, amps)))
    return pl.pallas_call(
        second_kernel,
        out_shape=(half, half),
        in_specs=[pl.BlockSpec(memory_space=pltpu.SMEM), in_vmem],
        out_specs=(in_vmem,) * 2,
        scratch_shapes=[acc],
        **params,
    )(table, pltpu.with_memory_space_constraint(amps, pltpu.VMEM))


def combine(body, outs, *arrays):
    in_vmem = pl.BlockSpec(memory_space=pltpu.VMEM)
    return pl.pallas_call(
        body,
        out_shape=tuple(pltpu.VMEM(shape, jnp.float32) for shape in outs),
        in_specs=[in_vmem] * len(arrays),
        out_specs=(in_vmem,) * len(outs),
        compiler_params=pltpu.CompilerParams(vmem_limit_bytes=4 << 20),
        name=body.__name__,
    )(*(pltpu.with_memory_space_constraint(array, pltpu.VMEM) for array in arrays))


def add_halves(keep, got, send_a, keep_a, send_b, keep_b):
    for low, out, distances in ((0, send_a, (1, 2)), (0, keep_a, (0, 3)), (1, send_b, (3, 2)), (1, keep_b, (0, 1))):
        for n, k in enumerate(distances):
            out[n] = keep[k, low] + got[k, low]


def add_first(keep_a, got_a, keep_b, got_b, own_a, send_a, own_b, send_b):
    own_a[...] = keep_a[0] + got_a[0]
    send_a[...] = keep_a[1] + got_a[1]
    own_b[...] = keep_b[0] + got_b[0]
    send_b[...] = keep_b[1] + got_b[1]


def add_ring(*refs):
    arrived, sums = refs[:8], refs[8:]
    swapped = (lax.axis_index("y") >> 1) ^ lax.axis_index("x_hi")
    for turn in range(2):

        @pl.when(swapped == turn)
        def _():
            for run in range(2):
                for low in range(2):
                    own, got = arrived[4 * run + 2 * low : 4 * run + 2 * low + 2]
                    sums[2 * (run ^ turn) + low][...] = own[...] + got[...]


def layout_kernel(scale, mine, other, out, whole):
    core = lax.axis_index("core")
    whole[pl.ds(core * 2 * UNIT, 2 * UNIT)] = mine[...] * scale
    whole[pl.ds((1 - core) * 2 * UNIT, 2 * UNIT)] = other[...] * scale
    for half in range(2):
        for m in range(FULL):
            g, l = divmod(m, WIDE)
            row = 8 * (half * HALF_GROUPS + g)
            out[0, row : row + 8, 128 * l : 128 * l + 128] = whole[half * 2 * UNIT + m]
        for g in range(HALF_GROUPS):
            n, k = divmod(g, 8)
            tile = whole[half * 2 * UNIT + FULL + n]
            if k:
                tile = pltpu.roll(tile, 128 - 16 * k, 1)
            row = 8 * (half * HALF_GROUPS + g)
            out[0, row : row + 8, 128 * WIDE : 128 * WIDE + 16] = tile[:, :16]


def lay_out(scale, size, *units):
    return pl.pallas_call(
        functools.partial(layout_kernel, scale),
        out_shape=jax.ShapeDtypeStruct((1, size, size), jnp.float32),
        in_specs=[pl.BlockSpec(memory_space=pltpu.VMEM)] * 2,
        out_specs=pl.BlockSpec(memory_space=pltpu.VMEM),
        scratch_shapes=[pltpu.VMEM((4 * UNIT, 8, 128), jnp.float32)],
        compiler_params=pltpu.CompilerParams(vmem_limit_bytes=8 << 20),
        name="lay_out",
    )(*(pltpu.with_memory_space_constraint(unit, pltpu.VMEM) for unit in units))


def on_device(amps, conserve):
    scale = 1.0 / (8 * 32 * amps.shape[3] * amps.shape[4])
    table, own = conserve[0, 0], amps[0, 0]
    blocks, keep, give = densities(0, table, own)
    runs = [(keep, send(give, across)), None]
    keep, give = densities(1, table, blocks)
    runs[1] = (keep, send(give, across))

    unit = (UNIT, 8, 128)
    begun = []
    for keep, got in runs:
        send_a, keep_a, send_b, keep_b = combine(add_halves, [(2, *unit)] * 4, keep, got)
        begun.append((keep_a, send(send_a, functools.partial(around, 1, 0)), keep_b, send(send_b, functools.partial(around, 3, 0))))
    arrived = []
    for halves in begun:
        own_a, send_a, own_b, send_b = combine(add_first, [unit] * 4, *halves)
        arrived += [own_a, send(send_a, functools.partial(around, 3, 0)), own_b, send(send_b, functools.partial(around, 1, 0))]
    second = combine(add_ring, [unit] * 4, *arrived)
    came = [send(second[j], functools.partial(around, j, 1)) for j in (2, 1, 3)]
    third = (second[0] + came[0]) + (came[1] + came[2])
    parts = lax.all_to_all(third.reshape(8, UNIT // 8, 8, 128), "z", 0, 0, tiled=True)
    eighth = jnp.sum(parts, axis=0, keepdims=True)
    mine = lax.all_to_all(jnp.broadcast_to(eighth, (16, *parts.shape[1:])), ("x_lo", "z"), 0, 0, tiled=True)
    mine = mine.reshape(2 * UNIT, 8, 128)
    return lay_out(scale, amps.shape[4], mine, send(mine, across))


def solution(mesh):
    fine = Mesh(mesh.devices.reshape(SIZES), FINE)
    ki, kj = ("x_hi", "y"), ("x_lo", "z", "core")
    return jax.shard_map(
        on_device,
        mesh=fine,
        in_specs=(P(ki, kj, None, None, None, None), P(ki, kj, None)),
        out_specs=P(ki, None, None),
        check_vma=False,
    )
```

```python
import functools
import jax
import jax.numpy as jnp
from jax import lax
from jax.experimental import pallas as pl
from jax.experimental.pallas import tpu as pltpu
from jax.sharding import Mesh, PartitionSpec as P

FINE = ("x_hi", "y", "x_lo", "z", "core")
SIZES = (2, 4, 2, 8, 2)
HALF_GROUPS, WIDE, UNIT = 25, 3, 40
FULL = HALF_GROUPS * WIDE


def position(x, y, z, core):
    x, y, z, core = x % 4, y % 4, z % 8, core % 2
    return (((x // 2 * 4 + y) * 2 + x % 2) * 8 + z) * 2 + core


def pairs(move):
    found = []
    for x in range(4):
        for y in range(4):
            for z in range(8):
                for core in range(2):
                    dx, dy, dz, dc = move(x, y, z, core)
                    found.append((position(x, y, z, core), position(x + dx, y + dy, z + dz, core + dc)))
    return found


def send(value, move):
    return lax.ppermute(value, FINE, pairs(move))


def across(x, y, z, core):
    return 0, 0, 0, 1


def around(step, turn, x, y, z, core):
    return (0, (y ^ step) - y, 0, 0) if core == turn else ((x ^ step) - x, 0, 0, 0)


def block_of(place):
    run, y = place // 4, place % 4
    return (y // 2 ^ run) * 4 + y


def place_of(block):
    y = block % 4
    return (block // 4 ^ y // 2) * 4 + y


def add_block(blocks, acc, keep, give, block, partner, arrive=None):
    size = blocks.shape[2]
    x_low = lax.axis_index("x_lo")
    x, y = lax.axis_index("x_hi") * 2 + x_low, lax.axis_index("y")
    core = lax.axis_index("core")
    total = None
    for o in range(blocks.shape[1]):
        if arrive is not None:
            arrive(o)
        own = blocks[block, o]
        turned = own.T
        mix = turned + turned - blocks[partner, o]
        part = jnp.dot(own, mix, preferred_element_type=jnp.float32)
        total = part if total is None else total + part
    acc[:, :size] = total

    lane = lax.broadcasted_iota(jnp.int32, (8, 128), 1)

    def tile_of(half, m):
        if m == UNIT * 2 - 1:
            return jnp.zeros((8, 128), jnp.float32)

        def read(g, l):
            row = pl.multiple_of(half * (8 * HALF_GROUPS) + 8 * g, 8)
            return acc[pl.ds(row, 8), 128 * l : 128 * l + 128]

        if m < FULL:
            return read(*divmod(m, WIDE))
        first = 8 * (m - FULL)
        tile = read(first, WIDE)
        for k in range(1, min(8, HALF_GROUPS - first)):
            tile = jnp.where(lane < 16 * k, tile, pltpu.roll(read(first + k, WIDE), 16 * k, 1))
        return tile

    high, dy = block // 4, (block % 4) ^ y
    for target, half in ((keep, core), (give, 1 - core)):
        for low in range(2):
            dx = (high * 2 + low) ^ x
            k = jnp.where(half == 0, dy, dx)
            j = jnp.where(half == 0, low ^ x_low, dy & 1)
            for n in range(UNIT):
                target[k, j, n] = tile_of(half, low * UNIT + n)


def first_kernel(table_in, amps, blocks, keep, give, acc, table, order, table_sem, sems):
    count = blocks.shape[0]

    def fetch(n):
        block = order[n]
        return pltpu.make_async_copy(amps.at[block], blocks.at[block], sems.at[n])

    order[0] = 0
    fetch(0).start()
    copy = pltpu.make_async_copy(table_in, table, table_sem)
    copy.start()
    copy.wait()
    n = 0
    for place in range(count):
        block = block_of(place)
        partner = table[block]
        other_place = place_of(partner)
        order[n] = block
        n = n + (other_place >= place).astype(jnp.int32)
        order[n] = partner
        n = n + (other_place > place).astype(jnp.int32)
    for n in range(1, count):
        fetch(n).start()

    for place in range(4):
        fetch(2 * place).wait()
        fetch(2 * place + 1).wait()
        block = block_of(place)
        add_block(blocks, acc.at[place % 2], keep, give, block, table[block])


def second_kernel(table, blocks, keep, give, acc):
    for i in range(4):
        block = block_of(4 + i)
        add_block(blocks, acc.at[i % 2], keep, give, block, table[block])


def densities(run, table, amps):
    half = pltpu.VMEM((4, 2, UNIT, 8, 128), jnp.float32)
    in_vmem = pl.BlockSpec(memory_space=pltpu.VMEM)
    acc = pltpu.VMEM((2, amps.shape[2], 512), jnp.float32)
    params = dict(
        compiler_params=pltpu.CompilerParams(vmem_limit_bytes=12 << 20),
        cost_estimate=pl.CostEstimate(flops=4 << 30, bytes_accessed=13 << 20, transcendentals=0),
        name="densities",
    )
    if run == 0:
        dma = pltpu.SemaphoreType.DMA
        return pl.pallas_call(
            first_kernel,
            out_shape=(pltpu.VMEM(amps.shape, amps.dtype), half, half),
            in_specs=[pl.BlockSpec(memory_space=pltpu.HBM)] * 2,
            out_specs=(in_vmem,) * 3,
            scratch_shapes=[acc, *[pltpu.SMEM((n,), table.dtype) for n in (8, 10)], dma, dma((8,))],
            **params,
        )(*(pltpu.with_memory_space_constraint(array, pltpu.HBM) for array in (table, amps)))
    return pl.pallas_call(
        second_kernel,
        out_shape=(half, half),
        in_specs=[pl.BlockSpec(memory_space=pltpu.SMEM), in_vmem],
        out_specs=(in_vmem,) * 2,
        scratch_shapes=[acc],
        **params,
    )(table, pltpu.with_memory_space_constraint(amps, pltpu.VMEM))


def combine(body, outs, *arrays):
    in_vmem = pl.BlockSpec(memory_space=pltpu.VMEM)
    return pl.pallas_call(
        body,
        out_shape=tuple(pltpu.VMEM(shape, jnp.float32) for shape in outs),
        in_specs=[in_vmem] * len(arrays),
        out_specs=(in_vmem,) * len(outs),
        compiler_params=pltpu.CompilerParams(vmem_limit_bytes=4 << 20),
        name=body.__name__,
    )(*(pltpu.with_memory_space_constraint(array, pltpu.VMEM) for array in arrays))


def add_halves(keep, got, send_a, keep_a, send_b, keep_b):
    for low, out, distances in ((0, send_a, (1, 2)), (0, keep_a, (0, 3)), (1, send_b, (3, 2)), (1, keep_b, (0, 1))):
        for n, k in enumerate(distances):
            out[n] = keep[k, low] + got[k, low]


def add_first(keep_a, got_a, keep_b, got_b, own_a, send_a, own_b, send_b):
    own_a[...] = keep_a[0] + got_a[0]
    send_a[...] = keep_a[1] + got_a[1]
    own_b[...] = keep_b[0] + got_b[0]
    send_b[...] = keep_b[1] + got_b[1]


def add_ring(*refs):
    arrived, sums = refs[:8], refs[8:]
    swapped = (lax.axis_index("y") >> 1) ^ lax.axis_index("x_hi")
    for turn in range(2):

        @pl.when(swapped == turn)
        def _():
            for run in range(2):
                for low in range(2):
                    own, got = arrived[4 * run + 2 * low : 4 * run + 2 * low + 2]
                    sums[2 * (run ^ turn) + low][...] = own[...] + got[...]


def layout_kernel(scale, own, tiles, *refs):
    out, rows, sem = refs[-3:]
    core = lax.axis_index("core")
    half = core if own else 1 - core
    for m in range(FULL):
        g, l = divmod(m, WIDE)
        rows[8 * g : 8 * g + 8, 128 * l : 128 * l + 128] = tiles[m] * scale
    for g in range(HALF_GROUPS):
        n, k = divmod(g, 8)
        tile = tiles[FULL + n] * scale
        if k:
            tile = pltpu.roll(tile, 128 - 16 * k, 1)
        rows[8 * g : 8 * g + 8, 128 * WIDE : 128 * WIDE + 16] = tile[:, :16]
    count = 8 * HALF_GROUPS
    copy = pltpu.make_async_copy(rows, out.at[0, pl.ds(pl.multiple_of(half * count, 8), count)], sem)
    copy.start()
    copy.wait()


def lay_out(scale, size, tiles, begun=None):
    in_hbm = pl.BlockSpec(memory_space=pltpu.HBM)
    arrays = [pltpu.with_memory_space_constraint(tiles, pltpu.VMEM)]
    if begun is not None:
        arrays.append(pltpu.with_memory_space_constraint(begun, pltpu.HBM))
    return pl.pallas_call(
        functools.partial(layout_kernel, scale, begun is None),
        out_shape=pltpu.HBM((1, size, size), jnp.float32),
        in_specs=[pl.BlockSpec(memory_space=pltpu.VMEM), in_hbm][: len(arrays)],
        out_specs=in_hbm,
        scratch_shapes=[pltpu.VMEM((8 * HALF_GROUPS, size), jnp.float32), pltpu.SemaphoreType.DMA],
        input_output_aliases={} if begun is None else {1: 0},
        compiler_params=pltpu.CompilerParams(vmem_limit_bytes=8 << 20),
        cost_estimate=pl.CostEstimate(flops=80000, bytes_accessed=700000, transcendentals=0),
        name="lay_out",
    )(*arrays)


def on_device(amps, conserve):
    scale = 1.0 / (8 * 32 * amps.shape[3] * amps.shape[4])
    table, own = conserve[0, 0], amps[0, 0]
    blocks, keep, give = densities(0, table, own)
    runs = [(keep, send(give, across)), None]
    keep, give = densities(1, table, blocks)
    runs[1] = (keep, send(give, across))

    unit = (UNIT, 8, 128)
    begun = []
    for keep, got in runs:
        send_a, keep_a, send_b, keep_b = combine(add_halves, [(2, *unit)] * 4, keep, got)
        begun.append((keep_a, send(send_a, functools.partial(around, 1, 0)), keep_b, send(send_b, functools.partial(around, 3, 0))))
    arrived = []
    for halves in begun:
        own_a, send_a, own_b, send_b = combine(add_first, [unit] * 4, *halves)
        arrived += [own_a, send(send_a, functools.partial(around, 3, 0)), own_b, send(send_b, functools.partial(around, 1, 0))]
    second = combine(add_ring, [unit] * 4, *arrived)
    came = [send(second[j], functools.partial(around, j, 1)) for j in (2, 1, 3)]
    third = (second[0] + came[0]) + (came[1] + came[2])
    parts = lax.all_to_all(third.reshape(8, UNIT // 8, 8, 128), "z", 0, 0, tiled=True)
    eighth = jnp.sum(parts, axis=0, keepdims=True)
    mine = lax.all_to_all(jnp.broadcast_to(eighth, (16, *parts.shape[1:])), ("x_lo", "z"), 0, 0, tiled=True)
    mine = mine.reshape(2 * UNIT, 8, 128)
    other = send(mine, across)
    return lay_out(scale, amps.shape[4], other, lay_out(scale, amps.shape[4], mine))


def solution(mesh):
    fine = Mesh(mesh.devices.reshape(SIZES), FINE)
    ki, kj = ("x_hi", "y"), ("x_lo", "z", "core")
    return jax.shard_map(
        on_device,
        mesh=fine,
        in_specs=(P(ki, kj, None, None, None, None), P(ki, kj, None)),
        out_specs=P(ki, None, None),
        check_vma=False,
    )
```

```python
import functools
import jax
import jax.numpy as jnp
from jax import lax
from jax.experimental import pallas as pl
from jax.experimental.pallas import tpu as pltpu
from jax.sharding import Mesh, PartitionSpec as P

FINE = ("x_hi", "y", "x_lo", "z", "core")
SIZES = (2, 4, 2, 8, 2)
HALF_GROUPS, WIDE, UNIT = 25, 3, 40
FULL = HALF_GROUPS * WIDE


def position(x, y, z, core):
    x, y, z, core = x % 4, y % 4, z % 8, core % 2
    return (((x // 2 * 4 + y) * 2 + x % 2) * 8 + z) * 2 + core


def pairs(move):
    found = []
    for x in range(4):
        for y in range(4):
            for z in range(8):
                for core in range(2):
                    dx, dy, dz, dc = move(x, y, z, core)
                    found.append((position(x, y, z, core), position(x + dx, y + dy, z + dz, core + dc)))
    return found


def send(value, move):
    return lax.ppermute(value, FINE, pairs(move))


def across(x, y, z, core):
    return 0, 0, 0, 1


def around(step, turn, x, y, z, core):
    return (0, (y ^ step) - y, 0, 0) if core == turn else ((x ^ step) - x, 0, 0, 0)


def block_of(place):
    run, y = place // 4, place % 4
    return (y // 2 ^ run) * 4 + y


def place_of(block):
    y = block % 4
    return (block // 4 ^ y // 2) * 4 + y


def add_block(blocks, acc, keep, give, block, partner, arrive=None):
    size = blocks.shape[2]
    x_low = lax.axis_index("x_lo")
    x, y = lax.axis_index("x_hi") * 2 + x_low, lax.axis_index("y")
    core = lax.axis_index("core")
    total = None
    for o in range(blocks.shape[1]):
        if arrive is not None:
            arrive(o)
        own = blocks[block, o]
        turned = own.T
        mix = turned + turned - blocks[partner, o]
        part = jnp.dot(own, mix, preferred_element_type=jnp.float32)
        total = part if total is None else total + part
    acc[:, :size] = total

    lane = lax.broadcasted_iota(jnp.int32, (8, 128), 1)

    def tile_of(half, m):
        if m == UNIT * 2 - 1:
            return jnp.zeros((8, 128), jnp.float32)

        def read(g, l):
            row = pl.multiple_of(half * (8 * HALF_GROUPS) + 8 * g, 8)
            return acc[pl.ds(row, 8), 128 * l : 128 * l + 128]

        if m < FULL:
            return read(*divmod(m, WIDE))
        first = 8 * (m - FULL)
        tile = read(first, WIDE)
        for k in range(1, min(8, HALF_GROUPS - first)):
            tile = jnp.where(lane < 16 * k, tile, pltpu.roll(read(first + k, WIDE), 16 * k, 1))
        return tile

    high, dy = block // 4, (block % 4) ^ y
    for target, half in ((keep, core), (give, 1 - core)):
        for low in range(2):
            dx = (high * 2 + low) ^ x
            k = jnp.where(half == 0, dy, dx)
            j = jnp.where(half == 0, low ^ x_low, dy & 1)
            for n in range(UNIT):
                target[k, j, n] = tile_of(half, low * UNIT + n)


def first_kernel(table_in, amps, blocks, keep, give, acc, table, order, table_sem, sems):
    count = blocks.shape[0]

    def fetch(n):
        block = order[n]
        return pltpu.make_async_copy(amps.at[block], blocks.at[block], sems.at[n])

    order[0] = 0
    fetch(0).start()
    copy = pltpu.make_async_copy(table_in, table, table_sem)
    copy.start()
    copy.wait()
    n = 0
    for place in range(count):
        block = block_of(place)
        partner = table[block]
        other_place = place_of(partner)
        order[n] = block
        n = n + (other_place >= place).astype(jnp.int32)
        order[n] = partner
        n = n + (other_place > place).astype(jnp.int32)
    for n in range(1, count):
        fetch(n).start()

    for place in range(4):
        fetch(2 * place).wait()
        fetch(2 * place + 1).wait()
        block = block_of(place)
        add_block(blocks, acc.at[place % 2], keep, give, block, table[block])


def second_kernel(table, blocks, keep, give, acc):
    for i in range(4):
        block = block_of(4 + i)
        add_block(blocks, acc.at[i % 2], keep, give, block, table[block])


def densities(run, table, amps):
    half = pltpu.VMEM((4, 2, UNIT, 8, 128), jnp.float32)
    in_vmem = pl.BlockSpec(memory_space=pltpu.VMEM)
    acc = pltpu.VMEM((2, amps.shape[2], 512), jnp.float32)
    params = dict(
        compiler_params=pltpu.CompilerParams(vmem_limit_bytes=12 << 20),
        cost_estimate=pl.CostEstimate(flops=4 << 30, bytes_accessed=13 << 20, transcendentals=0),
        name="densities",
    )
    if run == 0:
        dma = pltpu.SemaphoreType.DMA
        return pl.pallas_call(
            first_kernel,
            out_shape=(pltpu.VMEM(amps.shape, amps.dtype), half, half),
            in_specs=[pl.BlockSpec(memory_space=pltpu.HBM)] * 2,
            out_specs=(in_vmem,) * 3,
            scratch_shapes=[acc, *[pltpu.SMEM((n,), table.dtype) for n in (8, 10)], dma, dma((8,))],
            **params,
        )(*(pltpu.with_memory_space_constraint(array, pltpu.HBM) for array in (table, amps)))
    return pl.pallas_call(
        second_kernel,
        out_shape=(half, half),
        in_specs=[pl.BlockSpec(memory_space=pltpu.SMEM), in_vmem],
        out_specs=(in_vmem,) * 2,
        scratch_shapes=[acc],
        **params,
    )(table, pltpu.with_memory_space_constraint(amps, pltpu.VMEM))


def combine(body, outs, *arrays):
    in_vmem = pl.BlockSpec(memory_space=pltpu.VMEM)
    return pl.pallas_call(
        body,
        out_shape=tuple(pltpu.VMEM(shape, jnp.float32) for shape in outs),
        in_specs=[in_vmem] * len(arrays),
        out_specs=(in_vmem,) * len(outs),
        compiler_params=pltpu.CompilerParams(vmem_limit_bytes=4 << 20),
        name=body.__name__,
    )(*(pltpu.with_memory_space_constraint(array, pltpu.VMEM) for array in arrays))


def add_halves(keep, got, send_a, keep_a, send_b, keep_b):
    for low, out, distances in ((0, send_a, (1, 2)), (0, keep_a, (0, 3)), (1, send_b, (3, 2)), (1, keep_b, (0, 1))):
        for n, k in enumerate(distances):
            out[n] = keep[k, low] + got[k, low]


def add_first(keep_a, got_a, keep_b, got_b, own_a, send_a, own_b, send_b):
    own_a[...] = keep_a[0] + got_a[0]
    send_a[...] = keep_a[1] + got_a[1]
    own_b[...] = keep_b[0] + got_b[0]
    send_b[...] = keep_b[1] + got_b[1]


def add_ring(*refs):
    arrived, sums = refs[:8], refs[8:]
    swapped = (lax.axis_index("y") >> 1) ^ lax.axis_index("x_hi")
    for turn in range(2):

        @pl.when(swapped == turn)
        def _():
            for run in range(2):
                for low in range(2):
                    own, got = arrived[4 * run + 2 * low : 4 * run + 2 * low + 2]
                    sums[2 * (run ^ turn) + low][...] = own[...] + got[...]


def layout_kernel(scale, own, tiles, *refs):
    out, rows, sem = refs[-3:]
    core = lax.axis_index("core")
    half = core if own else 1 - core

    def lies(m):
        unit, n = divmod(m, UNIT)
        z, n = divmod(n, UNIT // 8)
        return (z * 2 + unit) * (UNIT // 8) + n

    for m in range(FULL):
        g, l = divmod(m, WIDE)
        rows[8 * g : 8 * g + 8, 128 * l : 128 * l + 128] = tiles[lies(m)] * scale
    for g in range(HALF_GROUPS):
        n, k = divmod(g, 8)
        tile = tiles[lies(FULL + n)] * scale
        if k:
            tile = pltpu.roll(tile, 128 - 16 * k, 1)
        rows[8 * g : 8 * g + 8, 128 * WIDE : 128 * WIDE + 16] = tile[:, :16]
    count = 8 * HALF_GROUPS
    copy = pltpu.make_async_copy(rows, out.at[0, pl.ds(pl.multiple_of(half * count, 8), count)], sem)
    copy.start()
    copy.wait()


def lay_out(scale, size, tiles, begun=None):
    in_hbm = pl.BlockSpec(memory_space=pltpu.HBM)
    arrays = [pltpu.with_memory_space_constraint(tiles, pltpu.VMEM)]
    if begun is not None:
        arrays.append(pltpu.with_memory_space_constraint(begun, pltpu.HBM))
    return pl.pallas_call(
        functools.partial(layout_kernel, scale, begun is None),
        out_shape=pltpu.HBM((1, size, size), jnp.float32),
        in_specs=[pl.BlockSpec(memory_space=pltpu.VMEM), in_hbm][: len(arrays)],
        out_specs=in_hbm,
        scratch_shapes=[pltpu.VMEM((8 * HALF_GROUPS, size), jnp.float32), pltpu.SemaphoreType.DMA],
        input_output_aliases={} if begun is None else {1: 0},
        compiler_params=pltpu.CompilerParams(vmem_limit_bytes=8 << 20),
        cost_estimate=pl.CostEstimate(flops=80000, bytes_accessed=700000, transcendentals=0),
        name="lay_out",
    )(*arrays)


def on_device(amps, conserve):
    scale = 1.0 / (8 * 32 * amps.shape[3] * amps.shape[4])
    table, own = conserve[0, 0], amps[0, 0]
    blocks, keep, give = densities(0, table, own)
    runs = [(keep, send(give, across)), None]
    keep, give = densities(1, table, blocks)
    runs[1] = (keep, send(give, across))

    unit = (UNIT, 8, 128)
    begun = []
    for keep, got in runs:
        send_a, keep_a, send_b, keep_b = combine(add_halves, [(2, *unit)] * 4, keep, got)
        begun.append((keep_a, send(send_a, functools.partial(around, 1, 0)), keep_b, send(send_b, functools.partial(around, 3, 0))))
    arrived = []
    for halves in begun:
        own_a, send_a, own_b, send_b = combine(add_first, [unit] * 4, *halves)
        arrived += [own_a, send(send_a, functools.partial(around, 3, 0)), own_b, send(send_b, functools.partial(around, 1, 0))]
    second = combine(add_ring, [unit] * 4, *arrived)
    came = [send(second[j], functools.partial(around, j, 1)) for j in (2, 1, 3)]
    third = (second[0] + came[0]) + (came[1] + came[2])
    parts = lax.all_to_all(third.reshape(8, UNIT // 8, 8, 128), "z", 0, 0, tiled=True)
    eighth = jnp.sum(parts, axis=0, keepdims=True)
    mine = lax.all_to_all(jnp.broadcast_to(eighth, (16, *parts.shape[1:])), ("z", "x_lo"), 0, 0, tiled=True)
    mine = mine.reshape(2 * UNIT, 8, 128)
    other = send(mine, across)
    return lay_out(scale, amps.shape[4], other, lay_out(scale, amps.shape[4], mine))


def solution(mesh):
    fine = Mesh(mesh.devices.reshape(SIZES), FINE)
    ki, kj = ("x_hi", "y"), ("x_lo", "z", "core")
    return jax.shard_map(
        on_device,
        mesh=fine,
        in_specs=(P(ki, kj, None, None, None, None), P(ki, kj, None)),
        out_specs=P(ki, None, None),
        check_vma=False,
    )
```

```python
import functools
import jax
import jax.numpy as jnp
from jax import lax
from jax.experimental import pallas as pl
from jax.experimental.pallas import tpu as pltpu
from jax.sharding import Mesh, PartitionSpec as P

FINE = ("x_hi", "y", "x_lo", "z", "core")
SIZES = (2, 4, 2, 8, 2)
HALF_GROUPS, WIDE, UNIT = 25, 3, 40
FULL = HALF_GROUPS * WIDE


def position(x, y, z, core):
    x, y, z, core = x % 4, y % 4, z % 8, core % 2
    return (((x // 2 * 4 + y) * 2 + x % 2) * 8 + z) * 2 + core


def pairs(move):
    found = []
    for x in range(4):
        for y in range(4):
            for z in range(8):
                for core in range(2):
                    dx, dy, dz, dc = move(x, y, z, core)
                    found.append((position(x, y, z, core), position(x + dx, y + dy, z + dz, core + dc)))
    return found


def send(value, move):
    return lax.ppermute(value, FINE, pairs(move))


def across(x, y, z, core):
    return 0, 0, 0, 1


def around(step, turn, x, y, z, core):
    return (0, (y ^ step) - y, 0, 0) if core == turn else ((x ^ step) - x, 0, 0, 0)


def block_of(place):
    run, y = place // 4, place % 4
    return (y // 2 ^ run) * 4 + y


def place_of(block):
    y = block % 4
    return (block // 4 ^ y // 2) * 4 + y


def add_block(blocks, acc, keep, give, block, partner, arrive=None):
    size = blocks.shape[2]
    x_low = lax.axis_index("x_lo")
    x, y = lax.axis_index("x_hi") * 2 + x_low, lax.axis_index("y")
    core = lax.axis_index("core")
    total = None
    for o in range(blocks.shape[1]):
        if arrive is not None:
            arrive(o)
        own = blocks[block, o]
        turned = own.T
        mix = turned + turned - blocks[partner, o]
        part = jnp.dot(own, mix, preferred_element_type=jnp.float32)
        total = part if total is None else total + part
    acc[:, :size] = total

    lane = lax.broadcasted_iota(jnp.int32, (8, 128), 1)

    def tile_of(half, m):
        if m == UNIT * 2 - 1:
            return jnp.zeros((8, 128), jnp.float32)

        def read(g, l):
            row = pl.multiple_of(half * (8 * HALF_GROUPS) + 8 * g, 8)
            return acc[pl.ds(row, 8), 128 * l : 128 * l + 128]

        if m < FULL:
            return read(*divmod(m, WIDE))
        first = 8 * (m - FULL)
        tile = read(first, WIDE)
        for k in range(1, min(8, HALF_GROUPS - first)):
            tile = jnp.where(lane < 16 * k, tile, pltpu.roll(read(first + k, WIDE), 16 * k, 1))
        return tile

    high, dy = block // 4, (block % 4) ^ y
    for target, half in ((keep, core), (give, 1 - core)):
        for low in range(2):
            dx = (high * 2 + low) ^ x
            k = jnp.where(half == 0, dy, dx)
            j = jnp.where(half == 0, low ^ x_low, dy & 1)
            for n in range(UNIT):
                target[k, j, n] = tile_of(half, low * UNIT + n)


def first_kernel(table_in, amps, blocks, keep, give, acc, table, order, table_sem, sems):
    count = blocks.shape[0]

    def fetch(n):
        block = order[n]
        return pltpu.make_async_copy(amps.at[block], blocks.at[block], sems.at[n])

    order[0] = 0
    fetch(0).start()
    copy = pltpu.make_async_copy(table_in, table, table_sem)
    copy.start()
    copy.wait()
    n = 0
    for place in range(count):
        block = block_of(place)
        partner = table[block]
        other_place = place_of(partner)
        order[n] = block
        n = n + (other_place >= place).astype(jnp.int32)
        order[n] = partner
        n = n + (other_place > place).astype(jnp.int32)
    for n in range(1, count):
        fetch(n).start()

    for place in range(4):
        fetch(2 * place).wait()
        fetch(2 * place + 1).wait()
        block = block_of(place)
        add_block(blocks, acc.at[place % 2], keep, give, block, table[block])


def second_kernel(table, blocks, keep, give, acc):
    for i in range(4):
        block = block_of(4 + i)
        add_block(blocks, acc.at[i % 2], keep, give, block, table[block])


def densities(run, table, amps):
    half = pltpu.VMEM((4, 2, UNIT, 8, 128), jnp.float32)
    in_vmem = pl.BlockSpec(memory_space=pltpu.VMEM)
    acc = pltpu.VMEM((2, amps.shape[2], 512), jnp.float32)
    params = dict(
        compiler_params=pltpu.CompilerParams(vmem_limit_bytes=12 << 20),
        cost_estimate=pl.CostEstimate(flops=4 << 30, bytes_accessed=13 << 20, transcendentals=0),
        name="densities",
    )
    if run == 0:
        dma = pltpu.SemaphoreType.DMA
        return pl.pallas_call(
            first_kernel,
            out_shape=(pltpu.VMEM(amps.shape, amps.dtype), half, half),
            in_specs=[pl.BlockSpec(memory_space=pltpu.HBM)] * 2,
            out_specs=(in_vmem,) * 3,
            scratch_shapes=[acc, *[pltpu.SMEM((n,), table.dtype) for n in (8, 10)], dma, dma((8,))],
            **params,
        )(*(pltpu.with_memory_space_constraint(array, pltpu.HBM) for array in (table, amps)))
    return pl.pallas_call(
        second_kernel,
        out_shape=(half, half),
        in_specs=[pl.BlockSpec(memory_space=pltpu.SMEM), in_vmem],
        out_specs=(in_vmem,) * 2,
        scratch_shapes=[acc],
        **params,
    )(table, pltpu.with_memory_space_constraint(amps, pltpu.VMEM))


def combine(body, outs, *arrays):
    in_vmem = pl.BlockSpec(memory_space=pltpu.VMEM)
    return pl.pallas_call(
        body,
        out_shape=tuple(pltpu.VMEM(shape, jnp.float32) for shape in outs),
        in_specs=[in_vmem] * len(arrays),
        out_specs=(in_vmem,) * len(outs),
        compiler_params=pltpu.CompilerParams(vmem_limit_bytes=4 << 20),
        name=body.__name__,
    )(*(pltpu.with_memory_space_constraint(array, pltpu.VMEM) for array in arrays))


def add_halves(keep, got, send_a, keep_a, send_b, keep_b):
    for low, out, distances in ((0, send_a, (1, 2)), (0, keep_a, (0, 3)), (1, send_b, (3, 2)), (1, keep_b, (0, 1))):
        for n, k in enumerate(distances):
            out[n] = keep[k, low] + got[k, low]


def add_first(keep_a, got_a, keep_b, got_b, own_a, send_a, own_b, send_b):
    own_a[...] = keep_a[0] + got_a[0]
    send_a[...] = keep_a[1] + got_a[1]
    own_b[...] = keep_b[0] + got_b[0]
    send_b[...] = keep_b[1] + got_b[1]


def add_ring(*refs):
    arrived, sums = refs[:8], refs[8:]
    swapped = (lax.axis_index("y") >> 1) ^ lax.axis_index("x_hi")
    for turn in range(2):

        @pl.when(swapped == turn)
        def _():
            for run in range(2):
                for low in range(2):
                    own, got = arrived[4 * run + 2 * low : 4 * run + 2 * low + 2]
                    sums[2 * (run ^ turn) + low][...] = own[...] + got[...]


def layout_kernel(scale, own, tiles, *refs):
    out, rows, sems = refs[-3:]
    core = lax.axis_index("core")
    half = core if own else 1 - core
    copies = []
    for part, groups in enumerate((range(16), range(16, HALF_GROUPS))):
        for g in groups:
            for l in range(WIDE):
                rows[8 * g : 8 * g + 8, 128 * l : 128 * l + 128] = tiles[g * WIDE + l] * scale
            n, k = divmod(g, 8)
            tile = tiles[FULL + n] * scale
            if k:
                tile = pltpu.roll(tile, 128 - 16 * k, 1)
            rows[8 * g : 8 * g + 8, 128 * WIDE : 128 * WIDE + 16] = tile[:, :16]
        first, count = 8 * groups[0], 8 * len(groups)
        there = pl.ds(pl.multiple_of(half * (8 * HALF_GROUPS) + first, 8), count)
        copies.append(pltpu.make_async_copy(rows.at[first : first + count], out.at[0, there], sems.at[part]))
        copies[-1].start()
    for copy in copies:
        copy.wait()


def lay_out(scale, size, tiles, begun=None):
    in_hbm = pl.BlockSpec(memory_space=pltpu.HBM)
    arrays = [pltpu.with_memory_space_constraint(tiles, pltpu.VMEM)]
    if begun is not None:
        arrays.append(pltpu.with_memory_space_constraint(begun, pltpu.HBM))
    return pl.pallas_call(
        functools.partial(layout_kernel, scale, begun is None),
        out_shape=pltpu.HBM((1, size, size), jnp.float32),
        in_specs=[pl.BlockSpec(memory_space=pltpu.VMEM), in_hbm][: len(arrays)],
        out_specs=in_hbm,
        scratch_shapes=[pltpu.VMEM((8 * HALF_GROUPS, size), jnp.float32), pltpu.SemaphoreType.DMA((2,))],
        input_output_aliases={} if begun is None else {1: 0},
        compiler_params=pltpu.CompilerParams(vmem_limit_bytes=8 << 20),
        cost_estimate=pl.CostEstimate(flops=80000, bytes_accessed=700000, transcendentals=0),
        name="lay_out",
    )(*arrays)


def on_device(amps, conserve):
    scale = 1.0 / (8 * 32 * amps.shape[3] * amps.shape[4])
    table, own = conserve[0, 0], amps[0, 0]
    blocks, keep, give = densities(0, table, own)
    runs = [(keep, send(give, across)), None]
    keep, give = densities(1, table, blocks)
    runs[1] = (keep, send(give, across))

    unit = (UNIT, 8, 128)
    begun = []
    for keep, got in runs:
        send_a, keep_a, send_b, keep_b = combine(add_halves, [(2, *unit)] * 4, keep, got)
        begun.append((keep_a, send(send_a, functools.partial(around, 1, 0)), keep_b, send(send_b, functools.partial(around, 3, 0))))
    arrived = []
    for halves in begun:
        own_a, send_a, own_b, send_b = combine(add_first, [unit] * 4, *halves)
        arrived += [own_a, send(send_a, functools.partial(around, 3, 0)), own_b, send(send_b, functools.partial(around, 1, 0))]
    second = combine(add_ring, [unit] * 4, *arrived)
    came = [send(second[j], functools.partial(around, j, 1)) for j in (2, 1, 3)]
    third = (second[0] + came[0]) + (came[1] + came[2])
    parts = lax.all_to_all(third.reshape(8, UNIT // 8, 8, 128), "z", 0, 0, tiled=True)
    eighth = jnp.sum(parts, axis=0, keepdims=True)
    mine = lax.all_to_all(jnp.broadcast_to(eighth, (16, *parts.shape[1:])), ("x_lo", "z"), 0, 0, tiled=True)
    mine = mine.reshape(2 * UNIT, 8, 128)
    other = send(mine, across)
    return lay_out(scale, amps.shape[4], other, lay_out(scale, amps.shape[4], mine))


def solution(mesh):
    fine = Mesh(mesh.devices.reshape(SIZES), FINE)
    ki, kj = ("x_hi", "y"), ("x_lo", "z", "core")
    return jax.shard_map(
        on_device,
        mesh=fine,
        in_specs=(P(ki, kj, None, None, None, None), P(ki, kj, None)),
        out_specs=P(ki, None, None),
        check_vma=False,
    )
```
